256 devices in a mesh: outer: 32 (over y_lo, z, core), inner: 8 (over y_hi, x).
Axes of the slice: x: 4, y: 4 (y_hi: 2, y_lo: 2; y = y_hi * 2 + y_lo), z: 8, core: 2. Of those that a mesh axis runs over, the one named last changes fastest.
Arguments:
- tokens: bfloat16 [180224, 4096], P(('outer', 'inner')), may hold values from -24 to 24
- weight: bfloat16 [4096, 512], P(('outer', 'inner')), may hold values from -0.09375 to 0.09375
- bias: float32 [512], replicated, may hold values from -5 to 5
- grad_values: bfloat16 [180224, 512], P(('outer', 'inner')), may hold values from -6 to 6
Outputs:
- values: bfloat16 [180224, 512], P(('outer', 'inner'))
- grad_tokens: bfloat16 [180224, 4096], P(('outer', 'inner'))
- grad_weight: float32 [4096, 512], P(('outer', 'inner'))
- grad_bias: float32 [512], replicated
The draws below stay inside these ranges and needn't reach their ends.
All inputs are finite; a program needn't handle non-finite values.
Results may differ from the reference program's by a relative error of at most 0.0005.
Values may be sent and summed in bfloat16 or wider, within the bound.
A program may use at most 128 MiB of HBM per device.

```python
import jax
import jax.numpy as jnp
from jax import lax

D = 4096
HV = 512
TOKENS = 180224


def spiked(array, stream_key, source, target, parts, factor):
    owner, partner = [(jnp.arange(array.shape[position]) // (array.shape[position] // parts)).reshape([-1 if axis == position else 1 for axis in range(array.ndim)]) for position in (source, target)]
    chosen = jax.random.permutation(stream_key, parts)[partner]
    strong = (owner == chosen) | (owner == (partner + parts // 2) % parts)
    return jnp.where(strong, factor * array, array)


def level_of(rng, dims, cuts, low, top_value):
    loudness = 1.0
    for dim, shards_of in cuts:
        steps = jax.random.uniform(jax.random.fold_in(jax.random.fold_in(rng, 6), dim), (shards_of,), jnp.float32, low / len(cuts), top_value / len(cuts))
        loudness = loudness * jnp.repeat(jnp.exp(steps), dims[dim] // shards_of).reshape((-1,) + (1,) * (len(dims) - 1 - dim))
    return loudness


def noise(stream_key, shape, spread, limit, shards=(), dtype=jnp.bfloat16):
    factor_of = level_of(stream_key, shape, shards, -0.22, 0.18) if shards else 1.0
    result = jax.random.normal(stream_key, shape, jnp.float32) * spread * factor_of
    return jnp.minimum(jnp.maximum(result, -limit), limit).astype(dtype)


def gaussian_with(rng, dims, width, bound, cuts, heavy, kind=jnp.bfloat16):
    array = width * jax.random.normal(rng, dims, jnp.float32)
    if cuts:
        array = array * level_of(rng, dims, cuts, -0.22, 0.18)
    return jnp.clip(spiked(array, jax.random.fold_in(rng, 3), *heavy), -bound, bound).astype(kind)


def setup_inputs(seed: int = 0) -> dict:
    key_of = jax.random.split(jax.random.key(seed), 5)
    tokens = gaussian_with(key_of[0], (TOKENS, D), 1.0, 24.0, ((0, 256),), (0, 1, 256, 6.0))
    weight = noise(key_of[1], (D, HV), D ** -0.5, 0.09375, ((0, 256),))
    bias = noise(key_of[2], (HV,), 1.0, 5.0, (), jnp.float32)
    grad_values = noise(key_of[3], (TOKENS, HV), 1.0, 6.0, ((0, 256),))
    return {"tokens": tokens, "weight": weight, "bias": bias, "grad_values": grad_values}


def reference(tokens, weight, bias, grad_values):
    scale = 1.0 / jnp.sqrt(jnp.float32(TOKENS))
    values = (jnp.dot(tokens, weight, preferred_element_type=jnp.float32) + bias).astype(jnp.bfloat16)
    grad_tokens = lax.dot_general(grad_values, weight, (((1,), (1,)), ((), ())), preferred_element_type=jnp.float32).astype(jnp.bfloat16)
    grad_weight = lax.dot_general(tokens, grad_values, (((0,), (0,)), ((), ())), preferred_element_type=jnp.float32) * scale
    grad_bias = lax.optimization_barrier(jnp.sum(grad_values.astype(jnp.float32), axis=0)) * scale
    return (values, grad_tokens, grad_weight, grad_bias)
```

```python
import functools

import jax
import jax.numpy as jnp
from jax import lax
from jax.experimental import pallas as pl
from jax.experimental.pallas import tpu as pltpu
from jax.sharding import PartitionSpec as P

X, Y, Z = 4, 4, 8
MESH = pl.DeviceIdType.MESH
F32, BF16 = jnp.float32, jnp.bfloat16
N_SEM = 170
LOW = (pl.ds(0, 4), pl.ds(0, 2), pl.ds(2, 1))
HIGH = (pl.ds(4, 4), pl.ds(0, 1), pl.ds(1, 2))
A_PARTS = ((pl.ds(0, 4), pl.ds(0, 2), pl.ds(0, 2)), (pl.ds(4, 4), pl.ds(0, 1), pl.ds(0, 1)))
B_PARTS = ((pl.ds(0, 4), pl.ds(2, 1), pl.ds(1, 1)), (pl.ds(4, 4), pl.ds(1, 2), pl.ds(0, 2)))
C_GROUP = pl.ds(3, 1)


def kernel(
    scale,
    tok_hbm, w_hbm, bias_ref, gv_hbm,
    val_hbm, gt_hbm, gw_ref, gb_ref,
    tok, gv, wb, gall, gr, acc, gto, valo,
    rx1, ry1, sa, sb, ry2, rx2, s2, rz3, cp, cm, sc, rc2, sc2, rc3,
    bb, bx, by, bz,
    ssem, rsem, dsem, drsem, lsem, osem,
):
    outer = lax.axis_index("outer")
    inner = lax.axis_index("inner")
    c = lax.rem(outer, 2)
    z = lax.rem(outer // 2, Z)
    yl = outer // (2 * Z)
    x = lax.rem(inner, X)
    yh = inner // X
    y = yh * 2 + yl

    def dev(px, py, pz, pc):
        return {
            "outer": (lax.rem(py, 2) * Z + pz) * 2 + pc,
            "inner": (py // 2) * X + px,
        }

    def at_x(k):
        p = lax.rem(x + k + X, X)
        return p, dev(p, y, z, c)

    def at_y(k):
        p = lax.rem(y + k + Y, Y)
        return p, dev(x, p, z, c)

    def at_z(k):
        p = lax.rem(z + k + Z, Z)
        return p, dev(x, y, p, c)

    sibling = dev(x, y, z, 1 - c)
    yhl = lambda p: (p // 2, lax.rem(p, 2))
    count = [0]
    sends = []

    def send(src, dst, to):
        i = count[0]
        count[0] += 1
        cp_ = pltpu.make_async_remote_copy(
            src_ref=src, dst_ref=dst, send_sem=ssem.at[i], recv_sem=rsem.at[i],
            device_id=to, device_id_type=MESH,
        )
        cp_.start()
        sends.append(cp_)
        return i

    def got(i, dst):
        pltpu.make_async_remote_copy(
            src_ref=dst, dst_ref=dst, send_sem=ssem.at[i], recv_sem=rsem.at[i],
            device_id=sibling, device_id_type=MESH,
        ).wait_recv()

    half = (1 - yl, yl)
    tok_in = []
    for h in range(2):
        cols = pl.ds(pl.multiple_of(half[h] * 2048, 2048), 2048)
        tok_in.append(pltpu.make_async_copy(tok_hbm.at[:, cols], tok.at[:, cols], lsem.at[h]))
    gv_in = pltpu.make_async_copy(gv_hbm, gv, lsem.at[2])
    w_in = [
        pltpu.make_async_copy(
            w_hbm.at[:, pl.ds(g * 128, 128)], wb.at[yl, z, c, yh, x, g], lsem.at[3 + g]
        )
        for g in range(4)
    ]
    for cp_ in w_in:
        cp_.start()
    gv_in.start()
    for cp_ in tok_in:
        cp_.start()

    barrier = pltpu.get_barrier_semaphore()
    peers = [at_x(k)[1] for k in range(1, X)] + [at_y(k)[1] for k in range(1, Y)]
    peers += [at_z(k)[1] for k in range(1, Z)] + [sibling]
    for p in peers:
        pl.semaphore_signal(barrier, inc=1, device_id=p, device_id_type=MESH)
    for cp_ in w_in:
        cp_.wait()
    pl.semaphore_wait(barrier, len(peers))

    ag1 = []
    for k in range(1, Z):
        ref = wb.at[yl, z, c, yh, x, pl.ds(0, 3)]
        ag1.append(send(ref, ref, at_z(k)[1]))
    agc1 = []
    for k in range(1, Y):
        ref = wb.at[yl, z, c, yh, x, C_GROUP]
        agc1.append(send(ref, ref, at_y(k)[1]))

    gv_in.wait()
    gvf = gv[...].astype(F32)
    bb[c] = jnp.sum(gvf.reshape(-1, 8, 512), axis=0)
    bias_core = send(bb.at[c], bb.at[c], sibling)

    def d2d(h, i):
        return pltpu.make_async_remote_copy(
            src_ref=gall.at[1 - c, half[h], i], dst_ref=gr.at[half[h], i],
            send_sem=dsem.at[h * Z + i], recv_sem=drsem.at[h * Z + i],
            device_id=sibling, device_id_type=MESH,
        )

    def grads(h, lo, hi):
        @pl.loop(lo, hi)
        def _(i):
            col = pl.multiple_of((half[h] * Z + i) * 256, 256)
            part = lax.dot_general(
                tok[:, pl.ds(col, 256)], gv[...], (((0,), (0,)), ((), ())),
                preferred_element_type=F32,
            ) * scale
            for g in range(4):
                gall[:, half[h], i, :, :, g] = part[:, g * 128:(g + 1) * 128].reshape(
                    2, 2, X, 16, 128
                )
            d2d(h, i).start()

    tok_in[0].wait()
    grads(0, 0, Z)

    for k in range(1, Z):
        got(ag1[k - 1], wb.at[yl, at_z(-k)[0], c, yh, x, pl.ds(0, 3)])
    ag2a, ag2b, agc2 = {}, {}, {}
    for k in range(1, Y):
        for q, (zs, gs, _) in enumerate(A_PARTS):
            ref = wb.at[yl, zs, c, yh, x, gs]
            ag2a[k, q] = send(ref, ref, at_y(k)[1])
    for k in range(1, X):
        for q, (zs, gs, _) in enumerate(B_PARTS):
            ref = wb.at[yl, zs, c, yh, x, gs]
            ag2b[k, q] = send(ref, ref, at_x(k)[1])
    for k in range(1, Y):
        ph, pw = yhl(at_y(-k)[0])
        got(agc1[k - 1], wb.at[pw, z, c, ph, x, C_GROUP])
    for k in range(1, X):
        ref = wb.at[:, z, c, :, x, C_GROUP]
        agc2[k] = send(ref, ref, at_x(k)[1])

    tok_in[1].wait()
    grads(1, 0, Z)

    fwd = []

    def relay(ref):
        fwd.append((send(ref, ref, sibling), ref))

    for k in range(1, Y):
        ph, pw = yhl(at_y(-k)[0])
        for q, (zs, gs, _) in enumerate(A_PARTS):
            got(ag2a[k, q], wb.at[pw, zs, c, ph, x, gs])
    a_slab = lambda p, q, cc: wb.at[:, A_PARTS[q][0], cc, :, p, A_PARTS[q][1]]
    b_slab = lambda p, q, cc: wb.at[yhl(p)[1], B_PARTS[q][0], cc, yhl(p)[0], :, B_PARTS[q][1]]
    c_slab = lambda p, cc: wb.at[:, p, cc, :, :, C_GROUP]
    ag3a, ag3b, agp, agm = {}, {}, {}, {}
    for k in range(1, X):
        for q in range(2):
            ref = a_slab(x, q, c)
            ag3a[k, q] = send(ref, ref, at_x(k)[1])
    for k in range(1, X):
        for q, (zs, gs, _) in enumerate(B_PARTS):
            got(ag2b[k, q], wb.at[yl, zs, c, yh, at_x(-k)[0], gs])
    for k in range(1, Y):
        for q in range(2):
            ref = b_slab(y, q, c)
            ag3b[k, q] = send(ref, ref, at_y(k)[1])
    for k in range(1, X):
        got(agc2[k], wb.at[:, z, c, :, at_x(-k)[0], C_GROUP])

    def gather_ring(s):
        ref = c_slab(at_z(1 - s)[0], c)
        agp[s] = send(ref, ref, at_z(1)[1])
        if s < 4:
            ref = c_slab(at_z(s - 1)[0], c)
            agm[s] = send(ref, ref, at_z(-1)[1])

    def gather_ring_got(s):
        got(agp[s], c_slab(at_z(-s)[0], c))
        if s < 4:
            got(agm[s], c_slab(at_z(s)[0], c))

    gather_ring(1)
    d2d_c = {}

    def relay_all(table, key, mk):
        table[key] = send(mk(c), mk(c), sibling)

    for q in range(2):
        relay_all(d2d_c, ("a", 0, q), lambda cc: a_slab(x, q, cc))
        relay_all(d2d_c, ("b", 0, q), lambda cc: b_slab(y, q, cc))
    relay_all(d2d_c, ("c", 0, 0), lambda cc: c_slab(z, cc))

    rsa, rsb, rsp, rsm = {}, {}, {}, {}

    def combine(h):
        @pl.loop(0, Z)
        def _(i):
            pltpu.make_async_remote_copy(
                src_ref=gr.at[half[h], i], dst_ref=gr.at[half[h], i],
                send_sem=dsem.at[h * Z + i], recv_sem=drsem.at[h * Z + i],
                device_id=sibling, device_id_type=MESH,
            ).wait_recv()
            gall[c, half[h], i] = gall[c, half[h], i] + gr[half[h], i]

    def ring_first(h):
        rsp[1, h] = send(gall.at[c, half[h], at_z(4)[0], :, :, C_GROUP], cp.at[0, h], at_z(1)[1])
        rsm[1, h] = send(gall.at[c, half[h], at_z(-3)[0], :, :, C_GROUP], cm.at[0, h], at_z(-1)[1])

    def ring_next(s, h):
        got(rsp[s - 1, h], cp.at[s - 2, h])
        cp[s - 2, h] = cp[s - 2, h] + gall[c, half[h], at_z(5 - s)[0], :, :, C_GROUP]
        rsp[s, h] = send(cp.at[s - 2, h], cp.at[s - 1, h], at_z(1)[1])
        if s < 4:
            got(rsm[s - 1, h], cm.at[s - 2, h])
            cm[s - 2, h] = cm[s - 2, h] + gall[c, half[h], at_z(s - 4)[0], :, :, C_GROUP]
            rsm[s, h] = send(cm.at[s - 2, h], cm.at[s - 1, h], at_z(-1)[1])

    def scatter_first(h):
        ring_first(h)
        for k in range(1, X):
            p, to = at_x(k)
            for q, (zs, gs, ls) in enumerate(A_PARTS):
                rsa[k, q, h] = send(
                    gall.at[c, half[h], zs, :, p, gs], rx1.at[x, half[h], zs, :, ls], to
                )
        for k in ((1, 3), (2,))[h]:
            p, to = at_y(k)
            ph, _ = yhl(p)
            for q, (zs, gs, ls) in enumerate(B_PARTS):
                rsb[k, q] = send(
                    gall.at[c, half[h], zs, ph, :, gs], ry1.at[y, zs, :, ls], to
                )

    combine(0)
    scatter_first(0)
    combine(1)
    scatter_first(1)

    got(bias_core, bb.at[1 - c])
    bx[x] = bb[0] + bb[1]
    bias_x = [send(bx.at[x], bx.at[x], at_x(k)[1]) for k in range(1, X)]

    for s in range(1, 5):
        gather_ring_got(s)
        if s < 4:
            gather_ring(s + 1)
        relay_all(d2d_c, ("c", -s, 0), lambda cc: c_slab(at_z(-s)[0], cc))
        if s < 4:
            relay_all(d2d_c, ("c", s, 0), lambda cc: c_slab(at_z(s)[0], cc))
        if s < 4:
            for q in range(2):
                got(ag3a[s, q], a_slab(at_x(-s)[0], q, c))
                relay_all(d2d_c, ("a", s, q), lambda cc: a_slab(at_x(-s)[0], q, cc))
                got(ag3b[s, q], b_slab(at_y(-s)[0], q, c))
                relay_all(d2d_c, ("b", s, q), lambda cc: b_slab(at_y(-s)[0], q, cc))
    for h in range(2):
        ring_next(2, h)
    for (kind, k, q), i in d2d_c.items():
        if kind == "a":
            got(i, a_slab(at_x(-k)[0], q, 1 - c))
        elif kind == "b":
            got(i, b_slab(at_y(-k)[0], q, 1 - c))
        else:
            got(i, c_slab(at_z(k)[0], 1 - c))

    acc[...] = jnp.broadcast_to(bias_ref[...], acc.shape)

    def product_out(j):
        cols = pl.ds(pl.multiple_of(j * 512, 512), 512)
        return pltpu.make_async_copy(gto.at[:, cols], gt_hbm.at[:, cols], osem.at[j])

    def products(lo, hi):
        @pl.loop(lo, hi)
        def _(j):
            zz = pl.multiple_of(lax.rem(j, 4) * 2, 2)
            w = jnp.concatenate(
                [wb[j // 4, pl.ds(zz, 2), :, :, :, g].reshape(512, 128) for g in range(4)], axis=1
            )
            cols = pl.ds(pl.multiple_of(j * 512, 512), 512)
            gto[:, cols] = lax.dot_general(
                gv[...], w, (((1,), (1,)), ((), ())), preferred_element_type=F32
            ).astype(BF16)
            product_out(j).start()
            acc[...] += jnp.dot(tok[:, cols], w, preferred_element_type=F32)

    products(0, 3)
    for h in range(2):
        ring_next(3, h)
    for k in range(1, X):
        got(bias_x[k - 1], bx.at[at_x(-k)[0]])
    by[y] = (bx[0] + bx[1]) + (bx[2] + bx[3])
    bias_y = [send(by.at[y], by.at[y], at_y(k)[1]) for k in range(1, Y)]
    products(3, 6)
    for h in range(2):
        ring_next(4, h)
    for k in range(1, Y):
        got(bias_y[k - 1], by.at[at_y(-k)[0]])
    bz[z] = (by[0] + by[1]) + (by[2] + by[3])
    bias_z = [send(bz.at[z], bz.at[z], at_z(k)[1]) for k in range(1, Z)]
    products(6, 8)
    valo[...] = acc[...].astype(BF16)
    val_out = pltpu.make_async_copy(valo, val_hbm, osem.at[8])
    val_out.start()

    rs2a, rs2b, rsc2 = {}, {}, {}
    for h in range(2):
        for k in range(1, X):
            for q, (zs, gs, ls) in enumerate(A_PARTS):
                got(rsa[k, q, h], rx1.at[at_x(-k)[0], half[h], zs, :, ls])
        for q, (zs, gs, ls) in enumerate(A_PARTS):
            total = gall[c, half[h], zs, :, x, gs]
            for k in range(1, X):
                total = total + rx1[at_x(-k)[0], half[h], zs, :, ls]
            sa[half[h], zs, :, ls] = total
        for k in ((1, 3), (2,))[h]:
            p, to = at_y(k)
            ph, _ = yhl(p)
            for q, (zs, gs, ls) in enumerate(A_PARTS):
                rs2a[k, q] = send(sa.at[half[h], zs, ph, ls], ry2.at[y, zs, ls], to)
    for k in range(1, Y):
        for q, (zs, gs, ls) in enumerate(B_PARTS):
            got(rsb[k, q], ry1.at[at_y(-k)[0], zs, :, ls])
    for q, (zs, gs, ls) in enumerate(B_PARTS):
        total = gall[c, yl, zs, yh, :, gs]
        for k in range(1, Y):
            total = total + ry1[at_y(-k)[0], zs, :, ls]
        sb[zs, :, ls] = total
    for k in range(1, X):
        p, to = at_x(k)
        for q, (zs, gs, ls) in enumerate(B_PARTS):
            rs2b[k, q] = send(sb.at[zs, p, ls], rx2.at[x, zs, ls], to)
    for h in range(2):
        got(rsp[4, h], cp.at[3, h])
        got(rsm[3, h], cm.at[2, h])
        sc[half[h]] = gall[c, half[h], z, :, :, 3] + cp[3, h, :, :, 0] + cm[2, h, :, :, 0]
    for k in range(1, X):
        p, to = at_x(k)
        rsc2[k] = send(sc.at[:, :, p], rc2.at[x], to)

    for k in range(1, Y):
        for q, (zs, gs, ls) in enumerate(A_PARTS):
            got(rs2a[k, q], ry2.at[at_y(-k)[0], zs, ls])
    for q, (zs, gs, ls) in enumerate(A_PARTS):
        total = sa[yl, zs, yh, ls]
        for k in range(1, Y):
            total = total + ry2[at_y(-k)[0], zs, ls]
        s2[zs, gs] = total
    for k in range(1, X):
        for q, (zs, gs, ls) in enumerate(B_PARTS):
            got(rs2b[k, q], rx2.at[at_x(-k)[0], zs, ls])
    for q, (zs, gs, ls) in enumerate(B_PARTS):
        total = sb[zs, x, ls]
        for k in range(1, X):
            total = total + rx2[at_x(-k)[0], zs, ls]
        s2[zs, gs] = total
    rs3 = {}
    for k in range(1, Z):
        p, to = at_z(k)
        rs3[k] = send(s2.at[p], rz3.at[z], to)
    for k in range(1, X):
        got(rsc2[k], rc2.at[at_x(-k)[0]])
    total = sc[:, :, x]
    for k in range(1, X):
        total = total + rc2[at_x(-k)[0]]
    sc2[...] = total
    rsc3 = {}
    for k in range(1, Y):
        p, to = at_y(k)
        ph, pw = yhl(p)
        rsc3[k] = send(sc2.at[pw, ph], rc3.at[y], to)

    for k in range(1, Z):
        got(bias_z[k - 1], bz.at[at_z(-k)[0]])
    total = bz[0]
    for k in range(1, Z):
        total = total + bz[k]
    gb_ref[...] = jnp.sum(total, axis=0, keepdims=True) * scale
    for k in range(1, Y):
        got(rsc3[k], rc3.at[at_y(-k)[0]])
    total = sc2[yl, yh]
    for k in range(1, Y):
        total = total + rc3[at_y(-k)[0]]
    gw_ref[:, pl.ds(384, 128)] = total
    for k in range(1, Z):
        got(rs3[k], rz3.at[at_z(-k)[0]])
    total = s2[z]
    for k in range(1, Z):
        total = total + rz3[at_z(-k)[0]]
    for g in range(3):
        gw_ref[:, pl.ds(g * 128, 128)] = total[g]

    val_out.wait()
    for j in range(8):
        product_out(j).wait()
    for cp_ in sends:
        cp_.wait_send()

    @pl.loop(0, 2 * Z)
    def _(i):
        pltpu.make_async_remote_copy(
            src_ref=gr.at[0, 0], dst_ref=gr.at[0, 0], send_sem=dsem.at[i], recv_sem=drsem.at[i],
            device_id=sibling, device_id_type=MESH,
        ).wait_send()
    assert count[0] <= N_SEM, count[0]


def shards(tokens, weight, bias, grad_values):
    rows, width = tokens.shape
    feats = weight.shape[1]
    n = lax.axis_size("outer") * lax.axis_size("inner")
    scale = float(1.0 / (rows * n) ** 0.5)
    anyspace = pl.BlockSpec(memory_space=pl.ANY)
    vmem = pl.BlockSpec(memory_space=pltpu.VMEM)
    tile = (16, 128)
    scratch = [
        ((rows, width), BF16),
        ((rows, feats), BF16),
        ((2, Z, 2, 2, X, 4) + tile, BF16),
        ((2, 2, Z, 2, X, 4) + tile, F32),
        ((2, Z, 2, X, 4) + tile, F32),
        ((rows, feats), F32),
        ((rows, width), BF16),
        ((rows, feats), BF16),
        ((X, 2, Z, 2, 2) + tile, F32),
        ((Y, Z, X, 2) + tile, F32),
        ((2, Z, 2, 2) + tile, F32),
        ((Z, X, 2) + tile, F32),
        ((Y, Z, 2) + tile, F32),
        ((X, Z, 2) + tile, F32),
        ((Z, 3) + tile, F32),
        ((Z, 3) + tile, F32),
        ((4, 2, 2, X, 1) + tile, F32),
        ((3, 2, 2, X, 1) + tile, F32),
        ((2, 2, X) + tile, F32),
        ((X, 2, 2) + tile, F32),
        ((2, 2) + tile, F32),
        ((Y,) + tile, F32),
        ((2, 8, feats), F32),
        ((X, 8, feats), F32),
        ((Y, 8, feats), F32),
        ((Z, 8, feats), F32),
    ]
    dma = pltpu.SemaphoreType.DMA
    values, grad_tokens, grad_weight, grad_bias = pl.pallas_call(
        functools.partial(kernel, scale),
        out_shape=(
            jax.ShapeDtypeStruct((rows, feats), BF16),
            jax.ShapeDtypeStruct((rows, width), BF16),
            jax.ShapeDtypeStruct(weight.shape, F32),
            jax.ShapeDtypeStruct((1, feats), F32),
        ),
        in_specs=[anyspace, anyspace, vmem, anyspace],
        out_specs=(anyspace, anyspace, vmem, vmem),
        scratch_shapes=[pltpu.VMEM(s, d) for s, d in scratch]
        + [dma((N_SEM,)), dma((N_SEM,)), dma((2 * Z,)), dma((2 * Z,)), dma((8,)), dma((16,))],
        compiler_params=pltpu.CompilerParams(
            collective_id=0, has_side_effects=True, vmem_limit_bytes=60 * 1024 * 1024
        ),
        cost_estimate=pl.CostEstimate(
            flops=6 * rows * width * feats, bytes_accessed=4 * rows * width, transcendentals=0
        ),
    )(tokens, weight, bias.reshape(1, feats), grad_values)
    return values, grad_tokens, grad_weight, grad_bias.reshape(feats)


def solution(mesh):
    in_specs = (
        P(("outer", "inner"), None),
        P(("outer", "inner"), None),
        P(),
        P(("outer", "inner"), None),
    )
    out_specs = (
        P(("outer", "inner"), None),
        P(("outer", "inner"), None),
        P(("outer", "inner"), None),
        P(),
    )
    return jax.shard_map(shards, mesh=mesh, in_specs=in_specs, out_specs=out_specs, check_vma=False)
```

```python
import functools

import jax
import jax.numpy as jnp
from jax import lax
from jax.experimental import pallas as pl
from jax.experimental.pallas import tpu as pltpu
from jax.sharding import PartitionSpec as P

X, Y, Z = 4, 4, 8
MESH = pl.DeviceIdType.MESH
F32, BF16 = jnp.float32, jnp.bfloat16
N_SEM = 240
A_PARTS = ((pl.ds(0, 6), pl.ds(0, 2)), (pl.ds(6, 2), pl.ds(0, 1)))
B_PARTS = (
    (pl.ds(0, 4), pl.ds(2, 1), pl.ds(1, 1)),
    (pl.ds(4, 2), pl.ds(2, 2), pl.ds(1, 2)),
    (pl.ds(6, 2), pl.ds(1, 3), pl.ds(0, 3)),
)
C_PLACES = pl.ds(0, 4)
G3 = pl.ds(3, 1)


def reversed_bits(i):
    return lax.rem(i, 2) * 4 + lax.rem(i // 2, 2) * 2 + i // 4


def kernel(
    scale,
    tok_hbm, w_hbm, bias_ref, gv_hbm,
    valo, gto, gw_ref, gb_ref,
    tok, gv, wb, gall, gr, acc,
    rx1, ry1, rz1, sa, sb, sc, ry2, rx2, rc2, s2, sc2, rz3, rc3,
    bb, bx, by, bz,
    ssem, rsem, dsem, drsem, lsem,
):
    outer = lax.axis_index("outer")
    inner = lax.axis_index("inner")
    c = lax.rem(outer, 2)
    z = lax.rem(outer // 2, Z)
    yl = outer // (2 * Z)
    x = lax.rem(inner, X)
    yh = inner // X
    y = yh * 2 + yl
    pz = reversed_bits(z)
    even = lax.rem(z, 2) == 0
    odd = lax.rem(z, 2) == 1

    def dev(px, py, pz_, pc):
        return {
            "outer": (lax.rem(py, 2) * Z + pz_) * 2 + pc,
            "inner": (py // 2) * X + px,
        }

    def at_x(k):
        p = lax.rem(x + k + X, X)
        return p, dev(p, y, z, c)

    def at_y(k):
        p = lax.rem(y + k + Y, Y)
        return p, dev(x, p, z, c)

    def at_z(k):
        p = lax.rem(z + k + Z, Z)
        return p, dev(x, y, p, c)

    def away(k):
        return (even, odd) if k % 2 == 0 else (odd, even)

    sibling = dev(x, y, z, 1 - c)
    yhl = lambda p: (p // 2, lax.rem(p, 2))
    count = [0]
    sends = []

    def only(when, act):
        if when is None:
            act()
        else:
            pl.when(when)(act)

    def send(src, dst, to, when=None):
        i = count[0]
        count[0] += 1
        cp_ = pltpu.make_async_remote_copy(
            src_ref=src, dst_ref=dst, send_sem=ssem.at[i], recv_sem=rsem.at[i],
            device_id=to, device_id_type=MESH,
        )
        only(when, lambda: cp_.start())
        sends.append((cp_, when))
        return i

    def got(i, dst, when=None):
        cp_ = pltpu.make_async_remote_copy(
            src_ref=dst, dst_ref=dst, send_sem=ssem.at[i], recv_sem=rsem.at[i],
            device_id=sibling, device_id_type=MESH,
        )
        only(when, lambda: cp_.wait_recv())

    half = (1 - yl, yl)
    tok_in = []
    for h in range(2):
        cols = pl.ds(pl.multiple_of(half[h] * 2048, 2048), 2048)
        tok_in.append(pltpu.make_async_copy(tok_hbm.at[:, cols], tok.at[:, cols], lsem.at[h]))
    gv_in = pltpu.make_async_copy(gv_hbm, gv, lsem.at[2])
    w_in = [
        pltpu.make_async_copy(
            w_hbm.at[:, pl.ds(g * 128, 128)], wb.at[yl, pz, c, yh, x, g], lsem.at[3 + g]
        )
        for g in range(4)
    ]
    barrier = pltpu.get_barrier_semaphore()
    peers = [at_z(k)[1] for k in range(1, Z)] + [at_x(k)[1] for k in range(1, X)]
    peers += [at_y(k)[1] for k in range(1, Y)] + [sibling]
    for p in peers:
        pl.semaphore_signal(barrier, inc=1, device_id=p, device_id_type=MESH)
    gv_in.start()
    tok_in[0].start()
    for cp_ in w_in:
        cp_.start()
    tok_in[1].start()

    def d2d(h, i):
        return pltpu.make_async_remote_copy(
            src_ref=gall.at[1 - c, half[h], i], dst_ref=gr.at[half[h], i],
            send_sem=dsem.at[h * Z + i], recv_sem=drsem.at[h * Z + i],
            device_id=sibling, device_id_type=MESH,
        )

    def grads(h, lo, hi, and_send):
        @pl.loop(lo, hi)
        def _(i):
            col = pl.multiple_of((half[h] * Z + reversed_bits(i)) * 256, 256)
            part = lax.dot_general(
                tok[:, pl.ds(col, 256)], gv[...], (((0,), (0,)), ((), ())),
                preferred_element_type=F32,
            ) * scale
            for g in range(4):
                gall[:, half[h], i, :, :, g] = part[:, g * 128:(g + 1) * 128].reshape(
                    2, 2, X, 16, 128
                )
            if and_send:
                d2d(h, i).start()

    gv_in.wait()
    tok_in[0].wait()
    grads(0, 0, 4, False)
    for cp_ in w_in:
        cp_.wait()
    pl.semaphore_wait(barrier, len(peers))

    own = lambda gs: wb.at[yl, pz, c, yh, x, gs]
    ag1, ag1o, agc1 = {}, {}, {}
    for k in range(1, Z):
        to = at_z(k)[1]
        ag1[k] = send(own(pl.ds(0, 3)), own(pl.ds(0, 3)), to)
        ag1o[k] = send(own(G3), own(G3), to, odd)
    for k in range(1, Y):
        agc1[k] = send(own(G3), own(G3), at_y(k)[1], even)

    @pl.loop(0, 4)
    def _(i):
        d2d(0, i).start()

    grads(0, 4, Z, True)

    def combine(h):
        @pl.loop(0, Z)
        def _(i):
            pltpu.make_async_remote_copy(
                src_ref=gr.at[half[h], i], dst_ref=gr.at[half[h], i],
                send_sem=dsem.at[h * Z + i], recv_sem=drsem.at[h * Z + i],
                device_id=sibling, device_id_type=MESH,
            ).wait_recv()
            gall[c, half[h], i] = gall[c, half[h], i] + gr[half[h], i]

    rsa, rsb, rsz = {}, {}, {}

    def scatter_first(h):
        for k in range(1, X):
            p, to = at_x(k)
            for q, (zs, gs) in enumerate(A_PARTS):
                rsa[k, q, h] = send(
                    gall.at[c, half[h], zs, :, p, gs], rx1.at[x, half[h], zs, :, gs], to
                )
        for k in ((1, 3), (2,))[h]:
            p, to = at_y(k)
            for q, (zs, gs, ls) in enumerate(B_PARTS):
                rsb[k, q] = send(
                    gall.at[c, half[h], zs, yhl(p)[0], :, gs], ry1.at[y, zs, :, ls], to
                )
        for k in range(1, Z):
            p, to = at_z(k)
            rsz[k, h] = send(
                gall.at[c, half[h], reversed_bits(p), :, :, G3], rz1.at[z, half[h]], to, away(k)[0]
            )

    combine(0)
    scatter_first(0)

    for k in range(1, Z):
        place = reversed_bits(at_z(-k)[0])
        got(ag1[k], wb.at[yl, place, c, yh, x, pl.ds(0, 3)])
        got(ag1o[k], wb.at[yl, place, c, yh, x, G3], away(k)[1])
    a_piece = lambda py, px, q: wb.at[
        yhl(py)[1], A_PARTS[q][0], c, yhl(py)[0], px, A_PARTS[q][1]
    ]
    b_piece = lambda py, px, q: wb.at[
        yhl(py)[1], B_PARTS[q][0], c, yhl(py)[0], px, B_PARTS[q][1]
    ]
    ag2a, ag2b, agc2, ag3a, ag3b, ag3c = {}, {}, {}, {}, {}, {}
    for k in range(1, Y):
        for q in range(2):
            ref = a_piece(y, x, q)
            ag2a[k, q] = send(ref, ref, at_y(k)[1])
    for k in range(1, X):
        for q in range(3):
            ref = b_piece(y, x, q)
            ag2b[k, q] = send(ref, ref, at_x(k)[1])
    for k in range(1, Y):
        ph, pw = yhl(at_y(-k)[0])
        got(agc1[k], wb.at[pw, pz, c, ph, x, G3], even)
    for k in range(1, X):
        ref = wb.at[:, pz, c, :, x, G3]
        agc2[k] = send(ref, ref, at_x(k)[1], even)

    def spread_a(m):
        for k in range(1, X):
            for q in range(2):
                ref = a_piece(at_y(-m)[0], x, q)
                ag3a[k, q, m] = send(ref, ref, at_x(k)[1])

    def spread_b(m):
        for k in range(1, Y):
            for q in range(3):
                ref = b_piece(y, at_x(-m)[0], q)
                ag3b[k, q, m] = send(ref, ref, at_y(k)[1])

    spread_a(0)
    spread_b(0)

    tok_in[1].wait()
    grads(1, 0, Z, True)
    gvf = gv[...].astype(F32)
    bb[c] = jnp.sum(gvf.reshape(-1, 8, 512), axis=0)
    bias_core = send(bb.at[c], bb.at[c], sibling)

    for m in range(1, X):
        for q in range(2):
            got(ag2a[m, q], a_piece(at_y(-m)[0], x, q))
        spread_a(m)
        for q in range(3):
            got(ag2b[m, q], b_piece(y, at_x(-m)[0], q))
        spread_b(m)
    for k in range(1, X):
        got(agc2[k], wb.at[:, pz, c, :, at_x(-k)[0], G3], even)
    c_slab = lambda p: wb.at[:, reversed_bits(p), c, :, :, G3]
    for k in range(1, Z):
        ag3c[k] = send(c_slab(z), c_slab(z), at_z(k)[1], even)

    combine(1)
    scatter_first(1)

    got(bias_core, bb.at[1 - c])
    bx[x] = bb[0] + bb[1]
    bias_x = [send(bx.at[x], bx.at[x], at_x(k)[1]) for k in range(1, X)]

    a_slab = lambda p, q, cc: wb.at[:, A_PARTS[q][0], cc, :, p, A_PARTS[q][1]]
    b_slab = lambda p, q, cc: wb.at[yhl(p)[1], B_PARTS[q][0], cc, yhl(p)[0], :, B_PARTS[q][1]]
    relay_a, relay_b = {}, {}

    def relay(ref):
        return send(ref, ref, sibling)

    for q in range(2):
        relay_a[0, q] = relay(a_slab(x, q, c))
    for q in range(3):
        relay_b[0, q] = relay(b_slab(y, q, c))
    for k in range(1, X):
        for q in range(2):
            for m in range(Y):
                got(ag3a[k, q, m], a_piece(at_y(-m)[0], at_x(-k)[0], q))
            relay_a[k, q] = relay(a_slab(at_x(-k)[0], q, c))
        for q in range(3):
            for m in range(X):
                got(ag3b[k, q, m], b_piece(at_y(-k)[0], at_x(-m)[0], q))
            relay_b[k, q] = relay(b_slab(at_y(-k)[0], q, c))
    for k in range(1, Z):
        got(ag3c[k], c_slab(at_z(-k)[0]), away(k)[0])
    c_all = lambda cc: wb.at[:, C_PLACES, cc, :, :, G3]
    relay_c = relay(c_all(c))

    for k in range(1, X):
        got(bias_x[k - 1], bx.at[at_x(-k)[0]])
    by[y] = (bx[0] + bx[1]) + (bx[2] + bx[3])
    bias_y = [send(by.at[y], by.at[y], at_y(k)[1]) for k in range(1, Y)]

    rs2a, rs2b, rsc2 = {}, {}, {}

    def second_a(h):
        for q, (zs, gs) in enumerate(A_PARTS):
            total = gall[c, half[h], zs, :, x, gs]
            for k in range(1, X):
                src = at_x(-k)[0]
                got(rsa[k, q, h], rx1.at[src, half[h], zs, :, gs])
                total = total + rx1[src, half[h], zs, :, gs]
            sa[half[h], zs, :, gs] = total
        for k in ((1, 3), (2,))[h]:
            p, to = at_y(k)
            for q, (zs, gs) in enumerate(A_PARTS):
                rs2a[k, q] = send(sa.at[half[h], zs, yhl(p)[0], gs], ry2.at[y, zs, gs], to)

    second_a(0)

    for k in range(X):
        for q in range(2):
            got(relay_a[k, q], a_slab(at_x(-k)[0], q, 1 - c))
        for q in range(3):
            got(relay_b[k, q], b_slab(at_y(-k)[0], q, 1 - c))
    got(relay_c, c_all(1 - c))
    acc[...] = jnp.broadcast_to(bias_ref[...], acc.shape)

    def products(lo, hi):
        @pl.loop(lo, hi)
        def _(j):
            q = lax.rem(j, 4)
            p = lax.rem(q, 2) * 2 + q // 2
            w = jnp.concatenate(
                [
                    jnp.concatenate(
                        [wb[j // 4, p + d, :, :, :, g].reshape(256, 128) for d in (0, 4)], axis=0
                    )
                    for g in range(4)
                ],
                axis=1,
            )
            cols = pl.ds(pl.multiple_of(j * 512, 512), 512)
            gto[:, cols] = lax.dot_general(
                gv[...], w, (((1,), (1,)), ((), ())), preferred_element_type=F32
            ).astype(BF16)
            acc[...] += jnp.dot(tok[:, cols], w, preferred_element_type=F32)

    products(0, 6)

    second_a(1)
    for q, (zs, gs, ls) in enumerate(B_PARTS):
        total = gall[c, yl, zs, yh, :, gs]
        for k in range(1, Y):
            src = at_y(-k)[0]
            got(rsb[k, q], ry1.at[src, zs, :, ls])
            total = total + ry1[src, zs, :, ls]
        sb[zs, :, ls] = total
    for k in range(1, X):
        p, to = at_x(k)
        for q, (zs, gs, ls) in enumerate(B_PARTS):
            rs2b[k, q] = send(sb.at[zs, p, ls], rx2.at[x, zs, ls], to)
    for k in range(1, Z):
        for h in range(2):
            got(rsz[k, h], rz1.at[at_z(-k)[0], half[h]], even)

    @pl.when(even)
    def _():
        total = gall[c, :, pz, :, :, G3]
        for k in range(1, Z):
            total = total + rz1[at_z(-k)[0]]
        sc[...] = total

    for k in range(1, X):
        p, to = at_x(k)
        rsc2[k] = send(sc.at[:, :, p], rc2.at[x], to, even)

    for k in range(1, Y):
        got(bias_y[k - 1], by.at[at_y(-k)[0]])
    bz[z] = (by[0] + by[1]) + (by[2] + by[3])
    bias_z = [send(bz.at[z], bz.at[z], at_z(k)[1]) for k in range(1, Z)]
    products(6, 8)

    for q, (zs, gs) in enumerate(A_PARTS):
        total = sa[yl, zs, yh, gs]
        for k in range(1, Y):
            src = at_y(-k)[0]
            got(rs2a[k, q], ry2.at[src, zs, gs])
            total = total + ry2[src, zs, gs]
        s2[zs, gs] = total
    for q, (zs, gs, ls) in enumerate(B_PARTS):
        total = sb[zs, x, ls]
        for k in range(1, X):
            src = at_x(-k)[0]
            got(rs2b[k, q], rx2.at[src, zs, ls])
            total = total + rx2[src, zs, ls]
        s2[zs, gs] = total
    rs3, rs3o, rsc3 = {}, {}, {}
    first3 = pl.ds(0, 3)
    for k in range(1, Z):
        p, to = at_z(k)
        place = reversed_bits(p)
        rs3[k] = send(s2.at[place, first3], rz3.at[z, first3], to)
        rs3o[k] = send(s2.at[place, G3], rz3.at[z, G3], to, away(k)[1])
    for k in range(1, X):
        got(rsc2[k], rc2.at[at_x(-k)[0]], even)

    @pl.when(even)
    def _():
        total = sc[:, :, x]
        for k in range(1, X):
            total = total + rc2[at_x(-k)[0]]
        sc2[...] = total

    for k in range(1, Y):
        p, to = at_y(k)
        ph, pw = yhl(p)
        rsc3[k] = send(sc2.at[pw, ph], rc3.at[y], to, even)
    valo[...] = acc[...].astype(BF16)

    for k in range(1, Z):
        got(bias_z[k - 1], bz.at[at_z(-k)[0]])
    total = bz[0]
    for k in range(1, Z):
        total = total + bz[k]
    gb_ref[...] = jnp.sum(total, axis=0, keepdims=True) * scale
    for k in range(1, Y):
        got(rsc3[k], rc3.at[at_y(-k)[0]], even)

    @pl.when(even)
    def _():
        total = sc2[yl, yh, 0]
        for k in range(1, Y):
            total = total + rc3[at_y(-k)[0], 0]
        gw_ref[:, pl.ds(384, 128)] = total

    for k in range(1, Z):
        got(rs3[k], rz3.at[at_z(-k)[0], first3])
        got(rs3o[k], rz3.at[at_z(-k)[0], G3], odd)
    total = s2[pz, first3]
    for k in range(1, Z):
        total = total + rz3[at_z(-k)[0], first3]
    for g in range(3):
        gw_ref[:, pl.ds(g * 128, 128)] = total[g]

    @pl.when(odd)
    def _():
        total = s2[pz, 3]
        for k in range(1, Z):
            total = total + rz3[at_z(-k)[0], 3]
        gw_ref[:, pl.ds(384, 128)] = total

    for cp_, when in sends:
        only(when, lambda: cp_.wait_send())

    @pl.loop(0, 2 * Z)
    def _(i):
        pltpu.make_async_remote_copy(
            src_ref=gr.at[0, 0], dst_ref=gr.at[0, 0], send_sem=dsem.at[i], recv_sem=drsem.at[i],
            device_id=sibling, device_id_type=MESH,
        ).wait_send()
    assert count[0] <= N_SEM, count[0]


def write_kernel(val, gt, gw, gb, val_out, gt_out, gw_out, gb_out, sem):
    copies = [pltpu.make_async_copy(val, val_out, sem.at[0])]
    rows = gt.shape[0] // 4
    for q in range(4):
        part = pl.ds(q * rows, rows)
        copies.append(pltpu.make_async_copy(gt.at[part], gt_out.at[part], sem.at[1 + q]))
    copies.append(pltpu.make_async_copy(gw, gw_out, sem.at[5]))
    copies.append(pltpu.make_async_copy(gb, gb_out, sem.at[6]))
    for cp_ in copies:
        cp_.start()
    for cp_ in copies:
        cp_.wait()


def shards(tokens, weight, bias, grad_values):
    rows, width = tokens.shape
    feats = weight.shape[1]
    n = lax.axis_size("outer") * lax.axis_size("inner")
    scale = float(1.0 / (rows * n) ** 0.5)
    anyspace = pl.BlockSpec(memory_space=pl.ANY)
    vmem = pl.BlockSpec(memory_space=pltpu.VMEM)
    tile = (16, 128)
    scratch = [
        ((rows, width), BF16),
        ((rows, feats), BF16),
        ((2, Z, 2, 2, X, 4) + tile, BF16),
        ((2, 2, Z, 2, X, 4) + tile, F32),
        ((2, Z, 2, X, 4) + tile, F32),
        ((rows, feats), F32),
        ((X, 2, Z, 2, 2) + tile, F32),
        ((Y, Z, X, 3) + tile, F32),
        ((Z, 2, 2, X, 1) + tile, F32),
        ((2, Z, 2, 2) + tile, F32),
        ((Z, X, 3) + tile, F32),
        ((2, 2, X, 1) + tile, F32),
        ((Y, Z, 2) + tile, F32),
        ((X, Z, 3) + tile, F32),
        ((X, 2, 2, 1) + tile, F32),
        ((Z, 4) + tile, F32),
        ((2, 2, 1) + tile, F32),
        ((Z, 4) + tile, F32),
        ((Y, 1) + tile, F32),
        ((2, 8, feats), F32),
        ((X, 8, feats), F32),
        ((Y, 8, feats), F32),
        ((Z, 8, feats), F32),
    ]
    dma = pltpu.SemaphoreType.DMA
    outs = (
        ((rows, feats), BF16),
        ((rows, width), BF16),
        (weight.shape, F32),
        ((1, feats), F32),
    )
    results = pl.pallas_call(
        functools.partial(kernel, scale),
        out_shape=tuple(pltpu.VMEM(s, d) for s, d in outs),
        in_specs=[anyspace, anyspace, vmem, anyspace],
        out_specs=(vmem,) * 4,
        scratch_shapes=[pltpu.VMEM(s, d) for s, d in scratch]
        + [dma((N_SEM,)), dma((N_SEM,)), dma((2 * Z,)), dma((2 * Z,)), dma((8,))],
        compiler_params=pltpu.CompilerParams(
            collective_id=0, has_side_effects=True, vmem_limit_bytes=50 * 1024 * 1024
        ),
        cost_estimate=pl.CostEstimate(
            flops=6 * rows * width * feats, bytes_accessed=4 * rows * width, transcendentals=0
        ),
        name="gather_scatter",
    )(tokens, weight, bias.reshape(1, feats), grad_values)
    values, grad_tokens, grad_weight, grad_bias = pl.pallas_call(
        write_kernel,
        out_shape=tuple(jax.ShapeDtypeStruct(s, d) for s, d in outs),
        in_specs=[vmem] * 4,
        out_specs=(anyspace,) * 4,
        scratch_shapes=[dma((8,))],
        compiler_params=pltpu.CompilerParams(vmem_limit_bytes=1024 * 1024),
        name="write",
    )(*[pltpu.with_memory_space_constraint(r, pltpu.VMEM) for r in results])
    return values, grad_tokens, grad_weight, grad_bias.reshape(feats)


def solution(mesh):
    in_specs = (
        P(("outer", "inner"), None),
        P(("outer", "inner"), None),
        P(),
        P(("outer", "inner"), None),
    )
    out_specs = (
        P(("outer", "inner"), None),
        P(("outer", "inner"), None),
        P(("outer", "inner"), None),
        P(),
    )
    return jax.shard_map(shards, mesh=mesh, in_specs=in_specs, out_specs=out_specs, check_vma=False)
```

```python
import functools

import jax
import jax.numpy as jnp
from jax import lax
from jax.experimental import pallas as pl
from jax.experimental.pallas import tpu as pltpu
from jax.sharding import PartitionSpec as P

X, Y, Z = 4, 4, 8
MESH = pl.DeviceIdType.MESH
F32, BF16 = jnp.float32, jnp.bfloat16
N_SEM = 260
A_PARTS = ((pl.ds(0, 6), pl.ds(0, 2)), (pl.ds(6, 2), pl.ds(0, 1)))
B_PARTS = (
    (pl.ds(0, 4), pl.ds(2, 1), pl.ds(1, 1)),
    (pl.ds(4, 2), pl.ds(2, 2), pl.ds(1, 2)),
    (pl.ds(6, 2), pl.ds(1, 3), pl.ds(0, 3)),
)
C_PLACES = pl.ds(0, 4)
G3 = pl.ds(3, 1)


TOP = 2.0 ** 15.5
LEAST = 2.0 ** -100
NORMAL = 2.0 ** -126


def tiles(v):
    return v.reshape(v.shape[:-2] + (2, 8, 128))


def largest(v):
    return jnp.max(jnp.abs(v).reshape(-1, 8, 128), axis=0)


def encode(v, inverse):
    r = (tiles(v) * inverse).reshape(v.shape)
    r2 = r * r
    r4 = r2 * r2
    r8 = r4 * r4
    return jnp.where(r < 0, -r8, r8).astype(BF16)


def decode(code, unit):
    v = code.astype(F32)
    r2 = lax.rsqrt(jnp.maximum(jnp.abs(v), NORMAL))
    r4 = lax.rsqrt(r2)
    root = r4 * lax.rsqrt(r4)
    return (tiles(jnp.where(v < 0, -root, root)) * unit).reshape(v.shape)


def reversed_bits(i):
    return lax.rem(i, 2) * 4 + lax.rem(i // 2, 2) * 2 + i // 4


def kernel(
    scale,
    tok_hbm, w_hbm, bias_ref, gv_hbm,
    valo, gto, gw_ref, gb_ref,
    tok, gv, wb, gall, gr, acc,
    rx1, ry1, rz1, sa, sb, sc, ry2, rx2, rc2, s2, sc2, rz3, rc3,
    code, ea, eb, u, ux, uy, uz, u2, u2y, u2x,
    bb, bx, by, bz,
    ssem, rsem, dsem, drsem, lsem,
):
    outer = lax.axis_index("outer")
    inner = lax.axis_index("inner")
    c = lax.rem(outer, 2)
    z = lax.rem(outer // 2, Z)
    yl = outer // (2 * Z)
    x = lax.rem(inner, X)
    yh = inner // X
    y = yh * 2 + yl
    pz = reversed_bits(z)
    even = lax.rem(z, 2) == 0
    odd = lax.rem(z, 2) == 1

    def dev(px, py, pz_, pc):
        return {
            "outer": (lax.rem(py, 2) * Z + pz_) * 2 + pc,
            "inner": (py // 2) * X + px,
        }

    def at_x(k):
        p = lax.rem(x + k + X, X)
        return p, dev(p, y, z, c)

    def at_y(k):
        p = lax.rem(y + k + Y, Y)
        return p, dev(x, p, z, c)

    def at_z(k):
        p = lax.rem(z + k + Z, Z)
        return p, dev(x, y, p, c)

    def away(k):
        return (even, odd) if k % 2 == 0 else (odd, even)

    sibling = dev(x, y, z, 1 - c)
    yhl = lambda p: (p // 2, lax.rem(p, 2))
    count = [0]
    sends = []

    def only(when, act):
        if when is None:
            act()
        else:
            pl.when(when)(act)

    def send(src, dst, to, when=None):
        i = count[0]
        count[0] += 1
        cp_ = pltpu.make_async_remote_copy(
            src_ref=src, dst_ref=dst, send_sem=ssem.at[i], recv_sem=rsem.at[i],
            device_id=to, device_id_type=MESH,
        )
        only(when, lambda: cp_.start())
        sends.append((cp_, when))
        return i

    def got(i, dst, when=None):
        cp_ = pltpu.make_async_remote_copy(
            src_ref=dst, dst_ref=dst, send_sem=ssem.at[i], recv_sem=rsem.at[i],
            device_id=sibling, device_id_type=MESH,
        )
        only(when, lambda: cp_.wait_recv())

    half = (1 - yl, yl)
    tok_in = []
    for h in range(2):
        cols = pl.ds(pl.multiple_of(half[h] * 2048, 2048), 2048)
        tok_in.append(pltpu.make_async_copy(tok_hbm.at[:, cols], tok.at[:, cols], lsem.at[h]))
    gv_in = pltpu.make_async_copy(gv_hbm, gv, lsem.at[2])
    w_in = [
        pltpu.make_async_copy(
            w_hbm.at[:, pl.ds(g * 128, 128)], wb.at[yl, pz, c, yh, x, g], lsem.at[3 + g]
        )
        for g in range(4)
    ]
    barrier = pltpu.get_barrier_semaphore()
    peers = [at_z(k)[1] for k in range(1, Z)] + [at_x(k)[1] for k in range(1, X)]
    peers += [at_y(k)[1] for k in range(1, Y)] + [sibling]
    for p in peers:
        pl.semaphore_signal(barrier, inc=1, device_id=p, device_id_type=MESH)
    gv_in.start()
    tok_in[0].start()
    for cp_ in w_in:
        cp_.start()
    tok_in[1].start()

    def d2d(h, i):
        return pltpu.make_async_remote_copy(
            src_ref=gall.at[1 - c, half[h], i], dst_ref=gr.at[half[h], i],
            send_sem=dsem.at[h * Z + i], recv_sem=drsem.at[h * Z + i],
            device_id=sibling, device_id_type=MESH,
        )

    def grads(h, lo, hi, and_send):
        @pl.loop(lo, hi)
        def _(i):
            col = pl.multiple_of((half[h] * Z + reversed_bits(i)) * 256, 256)
            part = lax.dot_general(
                tok[:, pl.ds(col, 256)], gv[...], (((0,), (0,)), ((), ())),
                preferred_element_type=F32,
            ) * scale
            for g in range(4):
                gall[:, half[h], i, :, :, g] = part[:, g * 128:(g + 1) * 128].reshape(
                    2, 2, X, 16, 128
                )
            if and_send:
                d2d(h, i).start()

    gv_in.wait()
    tok_in[0].wait()
    grads(0, 0, 4, False)
    for cp_ in w_in:
        cp_.wait()
    pl.semaphore_wait(barrier, len(peers))

    own = lambda gs: wb.at[yl, pz, c, yh, x, gs]
    ag1, ag1o, agc1 = {}, {}, {}
    for k in range(1, Z):
        to = at_z(k)[1]
        ag1[k] = send(own(pl.ds(0, 3)), own(pl.ds(0, 3)), to)
        ag1o[k] = send(own(G3), own(G3), to, odd)
    for k in range(1, Y):
        agc1[k] = send(own(G3), own(G3), at_y(k)[1], even)

    @pl.loop(0, 4)
    def _(i):
        d2d(0, i).start()

    grads(0, 4, Z, True)

    def combine(h):
        def add(i, top):
            pltpu.make_async_remote_copy(
                src_ref=gr.at[half[h], i], dst_ref=gr.at[half[h], i],
                send_sem=dsem.at[h * Z + i], recv_sem=drsem.at[h * Z + i],
                device_id=sibling, device_id_type=MESH,
            ).wait_recv()
            both = gall[c, half[h], i] + gr[half[h], i]
            gall[c, half[h], i] = both
            return jnp.maximum(top, largest(both))

        top = lax.fori_loop(0, Z, add, jnp.full((8, 128), LEAST, F32))
        u[h] = top * (1.0 / TOP)
        inverse = TOP / top

        @pl.loop(0, Z)
        def _(i):
            code[half[h], i] = encode(gall[c, half[h], i], inverse)

    rsa, rsb, rsz, rsu = {}, {}, {}, {}

    def scatter_first(h):
        for k in range(1, X):
            p, to = at_x(k)
            for q, (zs, gs) in enumerate(A_PARTS):
                rsa[k, q, h] = send(
                    code.at[half[h], zs, :, p, gs], rx1.at[x, half[h], zs, :, gs], to
                )
            rsu["x", k, h] = send(u.at[h], ux.at[x, h], to)
        for k in ((1, 3), (2,))[h]:
            p, to = at_y(k)
            for q, (zs, gs, ls) in enumerate(B_PARTS):
                rsb[k, q] = send(
                    code.at[half[h], zs, yhl(p)[0], :, gs], ry1.at[y, zs, :, ls], to
                )
            rsu["y", k] = send(u.at[h], uy.at[y], to)
        for k in range(1, Z):
            p, to = at_z(k)
            rsz[k, h] = send(
                code.at[half[h], reversed_bits(p), :, :, G3], rz1.at[z, half[h]], to, away(k)[0]
            )
            rsu["z", k, h] = send(u.at[h], uz.at[z, half[h]], to, away(k)[0])

    combine(0)
    scatter_first(0)

    for k in range(1, Z):
        place = reversed_bits(at_z(-k)[0])
        got(ag1[k], wb.at[yl, place, c, yh, x, pl.ds(0, 3)])
        got(ag1o[k], wb.at[yl, place, c, yh, x, G3], away(k)[1])
    a_piece = lambda py, px, q: wb.at[
        yhl(py)[1], A_PARTS[q][0], c, yhl(py)[0], px, A_PARTS[q][1]
    ]
    b_piece = lambda py, px, q: wb.at[
        yhl(py)[1], B_PARTS[q][0], c, yhl(py)[0], px, B_PARTS[q][1]
    ]
    ag2a, ag2b, agc2, ag3a, ag3b, ag3c = {}, {}, {}, {}, {}, {}
    for k in range(1, Y):
        for q in range(2):
            ref = a_piece(y, x, q)
            ag2a[k, q] = send(ref, ref, at_y(k)[1])
    for k in range(1, X):
        for q in range(3):
            ref = b_piece(y, x, q)
            ag2b[k, q] = send(ref, ref, at_x(k)[1])
    for k in range(1, Y):
        ph, pw = yhl(at_y(-k)[0])
        got(agc1[k], wb.at[pw, pz, c, ph, x, G3], even)
    for k in range(1, X):
        ref = wb.at[:, pz, c, :, x, G3]
        agc2[k] = send(ref, ref, at_x(k)[1], even)

    def spread_a(m):
        for k in range(1, X):
            for q in range(2):
                ref = a_piece(at_y(-m)[0], x, q)
                ag3a[k, q, m] = send(ref, ref, at_x(k)[1])

    def spread_b(m):
        for k in range(1, Y):
            for q in range(3):
                ref = b_piece(y, at_x(-m)[0], q)
                ag3b[k, q, m] = send(ref, ref, at_y(k)[1])

    spread_a(0)
    spread_b(0)

    tok_in[1].wait()
    grads(1, 0, Z, True)
    gvf = gv[...].astype(F32)
    bb[c] = jnp.sum(gvf.reshape(-1, 8, 512), axis=0)
    bias_core = send(bb.at[c], bb.at[c], sibling)

    combine(1)
    scatter_first(1)

    for m in range(1, X):
        for q in range(2):
            got(ag2a[m, q], a_piece(at_y(-m)[0], x, q))
        spread_a(m)
        for q in range(3):
            got(ag2b[m, q], b_piece(y, at_x(-m)[0], q))
        spread_b(m)
    for k in range(1, X):
        got(agc2[k], wb.at[:, pz, c, :, at_x(-k)[0], G3], even)
    c_slab = lambda p: wb.at[:, reversed_bits(p), c, :, :, G3]
    for k in range(1, Z):
        ag3c[k] = send(c_slab(z), c_slab(z), at_z(k)[1], even)

    got(bias_core, bb.at[1 - c])
    bx[x] = bb[0] + bb[1]
    bias_x = [send(bx.at[x], bx.at[x], at_x(k)[1]) for k in range(1, X)]

    rs2a, rs2b, rsc2 = {}, {}, {}

    def second_a(h):
        top = jnp.full((8, 128), LEAST, F32)
        for k in range(1, X):
            got(rsu["x", k, h], ux.at[at_x(-k)[0], h])
        for q, (zs, gs) in enumerate(A_PARTS):
            total = gall[c, half[h], zs, :, x, gs]
            for k in range(1, X):
                src = at_x(-k)[0]
                got(rsa[k, q, h], rx1.at[src, half[h], zs, :, gs])
                total = total + decode(rx1[src, half[h], zs, :, gs], ux[src, h])
            sa[half[h], zs, :, gs] = total
            top = jnp.maximum(top, largest(total))
        u2[h] = top * (1.0 / TOP)
        for zs, gs in A_PARTS:
            ea[half[h], zs, :, gs] = encode(sa[half[h], zs, :, gs], TOP / top)
        for k in ((1, 3), (2,))[h]:
            p, to = at_y(k)
            for q, (zs, gs) in enumerate(A_PARTS):
                rs2a[k, q] = send(ea.at[half[h], zs, yhl(p)[0], gs], ry2.at[y, zs, gs], to)
            rsu["y2", k] = send(u2.at[h], u2y.at[y], to)

    second_a(0)
    second_a(1)
    top = jnp.full((8, 128), LEAST, F32)
    for k in range(1, Y):
        got(rsu["y", k], uy.at[at_y(-k)[0]])
    for q, (zs, gs, ls) in enumerate(B_PARTS):
        total = gall[c, yl, zs, yh, :, gs]
        for k in range(1, Y):
            src = at_y(-k)[0]
            got(rsb[k, q], ry1.at[src, zs, :, ls])
            total = total + decode(ry1[src, zs, :, ls], uy[src])
        sb[zs, :, ls] = total
        top = jnp.maximum(top, largest(total))
    u2[2] = top * (1.0 / TOP)
    for zs, gs, ls in B_PARTS:
        eb[zs, :, ls] = encode(sb[zs, :, ls], TOP / top)
    for k in range(1, X):
        p, to = at_x(k)
        for q, (zs, gs, ls) in enumerate(B_PARTS):
            rs2b[k, q] = send(eb.at[zs, p, ls], rx2.at[x, zs, ls], to)
        rsu["x2", k] = send(u2.at[2], u2x.at[x], to)
    for k in range(1, Z):
        for h in range(2):
            got(rsz[k, h], rz1.at[at_z(-k)[0], half[h]], even)
            got(rsu["z", k, h], uz.at[at_z(-k)[0], half[h]], even)

    @pl.when(even)
    def _():
        for w in range(2):
            total = gall[c, w, pz, :, :, G3]
            for k in range(1, Z):
                src = at_z(-k)[0]
                total = total + decode(rz1[src, w], uz[src, w])
            sc[w] = total

    for k in range(1, X):
        p, to = at_x(k)
        rsc2[k] = send(sc.at[:, :, p], rc2.at[x], to, even)

    a_slab = lambda p, q, cc: wb.at[:, A_PARTS[q][0], cc, :, p, A_PARTS[q][1]]
    b_slab = lambda p, q, cc: wb.at[yhl(p)[1], B_PARTS[q][0], cc, yhl(p)[0], :, B_PARTS[q][1]]
    relay_a, relay_b = {}, {}

    def relay(ref):
        return send(ref, ref, sibling)

    for q in range(2):
        relay_a[0, q] = relay(a_slab(x, q, c))
    for q in range(3):
        relay_b[0, q] = relay(b_slab(y, q, c))
    for k in range(1, X):
        for q in range(2):
            for m in range(Y):
                got(ag3a[k, q, m], a_piece(at_y(-m)[0], at_x(-k)[0], q))
            relay_a[k, q] = relay(a_slab(at_x(-k)[0], q, c))
        for q in range(3):
            for m in range(X):
                got(ag3b[k, q, m], b_piece(at_y(-k)[0], at_x(-m)[0], q))
            relay_b[k, q] = relay(b_slab(at_y(-k)[0], q, c))
    for k in range(1, Z):
        got(ag3c[k], c_slab(at_z(-k)[0]), away(k)[0])
    c_all = lambda cc: wb.at[:, C_PLACES, cc, :, :, G3]
    relay_c = relay(c_all(c))

    for k in range(1, X):
        got(bias_x[k - 1], bx.at[at_x(-k)[0]])
    by[y] = (bx[0] + bx[1]) + (bx[2] + bx[3])
    bias_y = [send(by.at[y], by.at[y], at_y(k)[1]) for k in range(1, Y)]

    for k in range(X):
        for q in range(2):
            got(relay_a[k, q], a_slab(at_x(-k)[0], q, 1 - c))
        for q in range(3):
            got(relay_b[k, q], b_slab(at_y(-k)[0], q, 1 - c))
    got(relay_c, c_all(1 - c))
    acc[...] = jnp.broadcast_to(bias_ref[...], acc.shape)

    def products(lo, hi):
        @pl.loop(lo, hi)
        def _(j):
            q = lax.rem(j, 4)
            p = lax.rem(q, 2) * 2 + q // 2
            w = jnp.concatenate(
                [
                    jnp.concatenate(
                        [wb[j // 4, p + d, :, :, :, g].reshape(256, 128) for d in (0, 4)], axis=0
                    )
                    for g in range(4)
                ],
                axis=1,
            )
            cols = pl.ds(pl.multiple_of(j * 512, 512), 512)
            gto[:, cols] = lax.dot_general(
                gv[...], w, (((1,), (1,)), ((), ())), preferred_element_type=F32
            ).astype(BF16)
            acc[...] += jnp.dot(tok[:, cols], w, preferred_element_type=F32)

    products(0, 4)

    for k in range(1, Y):
        got(bias_y[k - 1], by.at[at_y(-k)[0]])
    bz[z] = (by[0] + by[1]) + (by[2] + by[3])
    bias_z = [send(bz.at[z], bz.at[z], at_z(k)[1]) for k in range(1, Z)]
    for k in range(1, Y):
        got(rsu["y2", k], u2y.at[at_y(-k)[0]])
    for q, (zs, gs) in enumerate(A_PARTS):
        total = sa[yl, zs, yh, gs]
        for k in range(1, Y):
            src = at_y(-k)[0]
            got(rs2a[k, q], ry2.at[src, zs, gs])
            total = total + decode(ry2[src, zs, gs], u2y[src])
        s2[zs, gs] = total
    for k in range(1, X):
        got(rsu["x2", k], u2x.at[at_x(-k)[0]])
    for q, (zs, gs, ls) in enumerate(B_PARTS):
        total = sb[zs, x, ls]
        for k in range(1, X):
            src = at_x(-k)[0]
            got(rs2b[k, q], rx2.at[src, zs, ls])
            total = total + decode(rx2[src, zs, ls], u2x[src])
        s2[zs, gs] = total
    rs3, rs3o, rsc3 = {}, {}, {}
    first3 = pl.ds(0, 3)
    for k in range(1, Z):
        p, to = at_z(k)
        place = reversed_bits(p)
        rs3[k] = send(s2.at[place, first3], rz3.at[z, first3], to)
        rs3o[k] = send(s2.at[place, G3], rz3.at[z, G3], to, away(k)[1])
    for k in range(1, X):
        got(rsc2[k], rc2.at[at_x(-k)[0]], even)

    @pl.when(even)
    def _():
        total = sc[:, :, x]
        for k in range(1, X):
            total = total + rc2[at_x(-k)[0]]
        sc2[...] = total

    for k in range(1, Y):
        p, to = at_y(k)
        ph, pw = yhl(p)
        rsc3[k] = send(sc2.at[pw, ph], rc3.at[y], to, even)
    products(4, 8)
    valo[...] = acc[...].astype(BF16)

    for k in range(1, Z):
        got(bias_z[k - 1], bz.at[at_z(-k)[0]])
    total = bz[0]
    for k in range(1, Z):
        total = total + bz[k]
    gb_ref[...] = jnp.sum(total, axis=0, keepdims=True) * scale
    for k in range(1, Y):
        got(rsc3[k], rc3.at[at_y(-k)[0]], even)

    @pl.when(even)
    def _():
        total = sc2[yl, yh, 0]
        for k in range(1, Y):
            total = total + rc3[at_y(-k)[0], 0]
        gw_ref[:, pl.ds(384, 128)] = total

    for k in range(1, Z):
        got(rs3[k], rz3.at[at_z(-k)[0], first3])
        got(rs3o[k], rz3.at[at_z(-k)[0], G3], odd)
    total = s2[pz, first3]
    for k in range(1, Z):
        total = total + rz3[at_z(-k)[0], first3]
    for g in range(3):
        gw_ref[:, pl.ds(g * 128, 128)] = total[g]

    @pl.when(odd)
    def _():
        total = s2[pz, 3]
        for k in range(1, Z):
            total = total + rz3[at_z(-k)[0], 3]
        gw_ref[:, pl.ds(384, 128)] = total

    for cp_, when in sends:
        only(when, lambda: cp_.wait_send())

    @pl.loop(0, 2 * Z)
    def _(i):
        pltpu.make_async_remote_copy(
            src_ref=gr.at[0, 0], dst_ref=gr.at[0, 0], send_sem=dsem.at[i], recv_sem=drsem.at[i],
            device_id=sibling, device_id_type=MESH,
        ).wait_send()
    assert count[0] <= N_SEM, count[0]


def write_kernel(val, gt, gw, gb, val_out, gt_out, gw_out, gb_out, sem):
    copies = [pltpu.make_async_copy(val, val_out, sem.at[0])]
    rows = gt.shape[0] // 4
    for q in range(4):
        part = pl.ds(q * rows, rows)
        copies.append(pltpu.make_async_copy(gt.at[part], gt_out.at[part], sem.at[1 + q]))
    copies.append(pltpu.make_async_copy(gw, gw_out, sem.at[5]))
    copies.append(pltpu.make_async_copy(gb, gb_out, sem.at[6]))
    for cp_ in copies:
        cp_.start()
    for cp_ in copies:
        cp_.wait()


def shards(tokens, weight, bias, grad_values):
    rows, width = tokens.shape
    feats = weight.shape[1]
    n = lax.axis_size("outer") * lax.axis_size("inner")
    scale = float(1.0 / (rows * n) ** 0.5)
    anyspace = pl.BlockSpec(memory_space=pl.ANY)
    vmem = pl.BlockSpec(memory_space=pltpu.VMEM)
    tile = (16, 128)
    scratch = [
        ((rows, width), BF16),
        ((rows, feats), BF16),
        ((2, Z, 2, 2, X, 4) + tile, BF16),
        ((2, 2, Z, 2, X, 4) + tile, F32),
        ((2, Z, 2, X, 4) + tile, F32),
        ((rows, feats), F32),
        ((X, 2, Z, 2, 2) + tile, BF16),
        ((Y, Z, X, 3) + tile, BF16),
        ((Z, 2, 2, X, 1) + tile, BF16),
        ((2, Z, 2, 2) + tile, F32),
        ((Z, X, 3) + tile, F32),
        ((2, 2, X, 1) + tile, F32),
        ((Y, Z, 2) + tile, BF16),
        ((X, Z, 3) + tile, BF16),
        ((X, 2, 2, 1) + tile, F32),
        ((Z, 4) + tile, F32),
        ((2, 2, 1) + tile, F32),
        ((Z, 4) + tile, F32),
        ((Y, 1) + tile, F32),
        ((2, Z, 2, X, 4) + tile, BF16),
        ((2, Z, 2, 2) + tile, BF16),
        ((Z, X, 3) + tile, BF16),
        ((2, 8, 128), F32),
        ((X, 2, 8, 128), F32),
        ((Y, 8, 128), F32),
        ((Z, 2, 8, 128), F32),
        ((3, 8, 128), F32),
        ((Y, 8, 128), F32),
        ((X, 8, 128), F32),
        ((2, 8, feats), F32),
        ((X, 8, feats), F32),
        ((Y, 8, feats), F32),
        ((Z, 8, feats), F32),
    ]
    dma = pltpu.SemaphoreType.DMA
    outs = (
        ((rows, feats), BF16),
        ((rows, width), BF16),
        (weight.shape, F32),
        ((1, feats), F32),
    )
    results = pl.pallas_call(
        functools.partial(kernel, scale),
        out_shape=tuple(pltpu.VMEM(s, d) for s, d in outs),
        in_specs=[anyspace, anyspace, vmem, anyspace],
        out_specs=(vmem,) * 4,
        scratch_shapes=[pltpu.VMEM(s, d) for s, d in scratch]
        + [dma((N_SEM,)), dma((N_SEM,)), dma((2 * Z,)), dma((2 * Z,)), dma((8,))],
        compiler_params=pltpu.CompilerParams(
            collective_id=0, has_side_effects=True, vmem_limit_bytes=50 * 1024 * 1024
        ),
        cost_estimate=pl.CostEstimate(
            flops=6 * rows * width * feats, bytes_accessed=4 * rows * width, transcendentals=0
        ),
        name="gather_scatter",
    )(tokens, weight, bias.reshape(1, feats), grad_values)
    values, grad_tokens, grad_weight, grad_bias = pl.pallas_call(
        write_kernel,
        out_shape=tuple(jax.ShapeDtypeStruct(s, d) for s, d in outs),
        in_specs=[vmem] * 4,
        out_specs=(anyspace,) * 4,
        scratch_shapes=[dma((8,))],
        compiler_params=pltpu.CompilerParams(vmem_limit_bytes=1024 * 1024),
        name="write",
    )(*[pltpu.with_memory_space_constraint(r, pltpu.VMEM) for r in results])
    return values, grad_tokens, grad_weight, grad_bias.reshape(feats)


def solution(mesh):
    in_specs = (
        P(("outer", "inner"), None),
        P(("outer", "inner"), None),
        P(),
        P(("outer", "inner"), None),
    )
    out_specs = (
        P(("outer", "inner"), None),
        P(("outer", "inner"), None),
        P(("outer", "inner"), None),
        P(),
    )
    return jax.shard_map(shards, mesh=mesh, in_specs=in_specs, out_specs=out_specs, check_vma=False)
```

```python
import functools

import jax
import jax.numpy as jnp
from jax import lax
from jax.experimental import pallas as pl
from jax.experimental.pallas import tpu as pltpu
from jax.sharding import PartitionSpec as P

X, Y, Z = 4, 4, 8
MESH = pl.DeviceIdType.MESH
F32, BF16 = jnp.float32, jnp.bfloat16
N_SEM = 260
A_PARTS = ((pl.ds(0, 6), pl.ds(0, 2)), (pl.ds(6, 2), pl.ds(0, 1)))
B_PARTS = (
    (pl.ds(0, 4), pl.ds(2, 1), pl.ds(1, 1)),
    (pl.ds(4, 2), pl.ds(2, 2), pl.ds(1, 2)),
    (pl.ds(6, 2), pl.ds(1, 3), pl.ds(0, 3)),
)
C_PLACES = pl.ds(0, 4)
G3 = pl.ds(3, 1)


TOP = 2.0 ** 15.5
LEAST = 2.0 ** -100
NORMAL = 2.0 ** -126


def tiles(v):
    return v.reshape(v.shape[:-2] + (2, 8, 128))


def largest(v):
    return jnp.max(jnp.abs(v).reshape(-1, 8, 128), axis=0)


def encode(v, inverse):
    r = (tiles(v) * inverse).reshape(v.shape)
    r2 = r * r
    r4 = r2 * r2
    r8 = r4 * r4
    return jnp.where(r < 0, -r8, r8).astype(BF16)


def decode(code, unit):
    v = code.astype(F32)
    r2 = lax.rsqrt(jnp.maximum(jnp.abs(v), NORMAL))
    r4 = lax.rsqrt(r2)
    root = r4 * lax.rsqrt(r4)
    return (tiles(jnp.where(v < 0, -root, root)) * unit).reshape(v.shape)


def reversed_bits(i):
    return lax.rem(i, 2) * 4 + lax.rem(i // 2, 2) * 2 + i // 4


def kernel(
    scale,
    tok_hbm, w_hbm, bias_ref, gv_hbm,
    valo, gto, gw_ref, gb_ref,
    tok, gv, wb, gall, gr, acc,
    rx1, ry1, rz1, sa, sb, sc, ry2, rx2, rc2, s2, sc2, rz3, rc3,
    code, ea, eb, u, ux, uy, uz, u2, u2y, u2x,
    bb, bx, by, bz,
    ssem, rsem, dsem, drsem, lsem,
):
    outer = lax.axis_index("outer")
    inner = lax.axis_index("inner")
    c = lax.rem(outer, 2)
    z = lax.rem(outer // 2, Z)
    yl = outer // (2 * Z)
    x = lax.rem(inner, X)
    yh = inner // X
    y = yh * 2 + yl
    pz = reversed_bits(z)
    even = lax.rem(z, 2) == 0
    odd = lax.rem(z, 2) == 1

    def dev(px, py, pz_, pc):
        return {
            "outer": (lax.rem(py, 2) * Z + pz_) * 2 + pc,
            "inner": (py // 2) * X + px,
        }

    def at_x(k):
        p = lax.rem(x + k + X, X)
        return p, dev(p, y, z, c)

    def at_y(k):
        p = lax.rem(y + k + Y, Y)
        return p, dev(x, p, z, c)

    def at_z(k):
        p = lax.rem(z + k + Z, Z)
        return p, dev(x, y, p, c)

    def away(k):
        return (even, odd) if k % 2 == 0 else (odd, even)

    sibling = dev(x, y, z, 1 - c)
    yhl = lambda p: (p // 2, lax.rem(p, 2))
    count = [0]
    sends = []

    def only(when, act):
        if when is None:
            act()
        else:
            pl.when(when)(act)

    def send(src, dst, to, when=None):
        i = count[0]
        count[0] += 1
        cp_ = pltpu.make_async_remote_copy(
            src_ref=src, dst_ref=dst, send_sem=ssem.at[i], recv_sem=rsem.at[i],
            device_id=to, device_id_type=MESH,
        )
        only(when, lambda: cp_.start())
        sends.append((cp_, when))
        return i

    def got(i, dst, when=None):
        cp_ = pltpu.make_async_remote_copy(
            src_ref=dst, dst_ref=dst, send_sem=ssem.at[i], recv_sem=rsem.at[i],
            device_id=sibling, device_id_type=MESH,
        )
        only(when, lambda: cp_.wait_recv())

    half = (1 - yl, yl)
    tok_in = []
    for h in range(2):
        cols = pl.ds(pl.multiple_of(half[h] * 2048, 2048), 2048)
        tok_in.append(pltpu.make_async_copy(tok_hbm.at[:, cols], tok.at[:, cols], lsem.at[h]))
    gv_in = pltpu.make_async_copy(gv_hbm, gv, lsem.at[2])
    w_in = [
        pltpu.make_async_copy(
            w_hbm.at[:, pl.ds(g * 128, 128)], wb.at[yl, pz, c, yh, x, g], lsem.at[3 + g]
        )
        for g in range(4)
    ]
    for cp_ in w_in:
        cp_.start()
    barrier = pltpu.get_barrier_semaphore()
    peers = [at_z(k)[1] for k in range(1, Z)] + [at_x(k)[1] for k in range(1, X)]
    peers += [at_y(k)[1] for k in range(1, Y)] + [sibling]
    for p in peers:
        pl.semaphore_signal(barrier, inc=1, device_id=p, device_id_type=MESH)
    gv_in.start()
    tok_in[0].start()
    tok_in[1].start()

    def d2d(h, i):
        return pltpu.make_async_remote_copy(
            src_ref=gall.at[1 - c, half[h], i], dst_ref=gr.at[half[h], i],
            send_sem=dsem.at[h * Z + i], recv_sem=drsem.at[h * Z + i],
            device_id=sibling, device_id_type=MESH,
        )

    def grads(h):
        @pl.loop(0, Z)
        def _(i):
            col = pl.multiple_of((half[h] * Z + reversed_bits(i)) * 256, 256)
            part = lax.dot_general(
                tok[:, pl.ds(col, 256)], gv[...], (((0,), (0,)), ((), ())),
                preferred_element_type=F32,
            ) * scale
            for g in range(4):
                gall[:, half[h], i, :, :, g] = part[:, g * 128:(g + 1) * 128].reshape(
                    2, 2, X, 16, 128
                )
            d2d(h, i).start()

    for cp_ in w_in:
        cp_.wait()
    pl.semaphore_wait(barrier, len(peers))

    own = lambda gs: wb.at[yl, pz, c, yh, x, gs]
    ag1, ag1o, agc1 = {}, {}, {}
    for k in range(1, Z):
        to = at_z(k)[1]
        ag1[k] = send(own(pl.ds(0, 3)), own(pl.ds(0, 3)), to)
        ag1o[k] = send(own(G3), own(G3), to, odd)
    for k in range(1, Y):
        agc1[k] = send(own(G3), own(G3), at_y(k)[1], even)

    gv_in.wait()
    tok_in[0].wait()
    grads(0)

    def combine(h):
        def add(i, top):
            pltpu.make_async_remote_copy(
                src_ref=gr.at[half[h], i], dst_ref=gr.at[half[h], i],
                send_sem=dsem.at[h * Z + i], recv_sem=drsem.at[h * Z + i],
                device_id=sibling, device_id_type=MESH,
            ).wait_recv()
            both = gall[c, half[h], i] + gr[half[h], i]
            gall[c, half[h], i] = both
            return jnp.maximum(top, largest(both))

        top = lax.fori_loop(0, Z, add, jnp.full((8, 128), LEAST, F32))
        u[h] = top * (1.0 / TOP)
        inverse = TOP / top

        @pl.loop(0, Z)
        def _(i):
            code[half[h], i] = encode(gall[c, half[h], i], inverse)

    rsa, rsb, rsz, rsu = {}, {}, {}, {}

    def scatter_first(h):
        for k in range(1, X):
            p, to = at_x(k)
            for q, (zs, gs) in enumerate(A_PARTS):
                rsa[k, q, h] = send(
                    code.at[half[h], zs, :, p, gs], rx1.at[x, half[h], zs, :, gs], to
                )
            rsu["x", k, h] = send(u.at[h], ux.at[x, h], to)
        for k in ((1, 3), (2,))[h]:
            p, to = at_y(k)
            for q, (zs, gs, ls) in enumerate(B_PARTS):
                rsb[k, q] = send(
                    code.at[half[h], zs, yhl(p)[0], :, gs], ry1.at[y, zs, :, ls], to
                )
            rsu["y", k] = send(u.at[h], uy.at[y], to)
        for k in range(1, Z):
            p, to = at_z(k)
            rsz[k, h] = send(
                code.at[half[h], reversed_bits(p), :, :, G3], rz1.at[z, half[h]], to, away(k)[0]
            )
            rsu["z", k, h] = send(u.at[h], uz.at[z, half[h]], to, away(k)[0])

    combine(0)
    scatter_first(0)

    for k in range(1, Z):
        place = reversed_bits(at_z(-k)[0])
        got(ag1[k], wb.at[yl, place, c, yh, x, pl.ds(0, 3)])
        got(ag1o[k], wb.at[yl, place, c, yh, x, G3], away(k)[1])
    a_piece = lambda py, px, q: wb.at[
        yhl(py)[1], A_PARTS[q][0], c, yhl(py)[0], px, A_PARTS[q][1]
    ]
    b_piece = lambda py, px, q: wb.at[
        yhl(py)[1], B_PARTS[q][0], c, yhl(py)[0], px, B_PARTS[q][1]
    ]
    ag2a, ag2b, agc2, ag3a, ag3b, ag3c = {}, {}, {}, {}, {}, {}
    for k in range(1, Y):
        for q in range(2):
            ref = a_piece(y, x, q)
            ag2a[k, q] = send(ref, ref, at_y(k)[1])
    for k in range(1, X):
        for q in range(3):
            ref = b_piece(y, x, q)
            ag2b[k, q] = send(ref, ref, at_x(k)[1])
    for k in range(1, Y):
        ph, pw = yhl(at_y(-k)[0])
        got(agc1[k], wb.at[pw, pz, c, ph, x, G3], even)
    for k in range(1, X):
        ref = wb.at[:, pz, c, :, x, G3]
        agc2[k] = send(ref, ref, at_x(k)[1], even)

    def spread_a(m):
        for k in range(1, X):
            for q in range(2):
                ref = a_piece(at_y(-m)[0], x, q)
                ag3a[k, q, m] = send(ref, ref, at_x(k)[1])

    def spread_b(m):
        for k in range(1, Y):
            for q in range(3):
                ref = b_piece(y, at_x(-m)[0], q)
                ag3b[k, q, m] = send(ref, ref, at_y(k)[1])

    spread_a(0)
    spread_b(0)

    tok_in[1].wait()
    grads(1)
    gvf = gv[...].astype(F32)
    bb[c] = jnp.sum(gvf.reshape(-1, 8, 512), axis=0)
    bias_core = send(bb.at[c], bb.at[c], sibling)

    combine(1)
    scatter_first(1)

    for m in range(1, X):
        for q in range(2):
            got(ag2a[m, q], a_piece(at_y(-m)[0], x, q))
        spread_a(m)
        for q in range(3):
            got(ag2b[m, q], b_piece(y, at_x(-m)[0], q))
        spread_b(m)
    for k in range(1, X):
        got(agc2[k], wb.at[:, pz, c, :, at_x(-k)[0], G3], even)
    c_slab = lambda p: wb.at[:, reversed_bits(p), c, :, :, G3]
    for k in range(1, Z):
        ag3c[k] = send(c_slab(z), c_slab(z), at_z(k)[1], even)

    got(bias_core, bb.at[1 - c])
    bx[x] = bb[0] + bb[1]
    bias_x = [send(bx.at[x], bx.at[x], at_x(k)[1]) for k in range(1, X)]

    rs2a, rs2b, rsc2 = {}, {}, {}

    def second_a(h):
        top = jnp.full((8, 128), LEAST, F32)
        for k in range(1, X):
            got(rsu["x", k, h], ux.at[at_x(-k)[0], h])
        for q, (zs, gs) in enumerate(A_PARTS):
            total = gall[c, half[h], zs, :, x, gs]
            for k in range(1, X):
                src = at_x(-k)[0]
                got(rsa[k, q, h], rx1.at[src, half[h], zs, :, gs])
                total = total + decode(rx1[src, half[h], zs, :, gs], ux[src, h])
            sa[half[h], zs, :, gs] = total
            top = jnp.maximum(top, largest(total))
        u2[h] = top * (1.0 / TOP)
        for zs, gs in A_PARTS:
            ea[half[h], zs, :, gs] = encode(sa[half[h], zs, :, gs], TOP / top)
        for k in ((1, 3), (2,))[h]:
            p, to = at_y(k)
            for q, (zs, gs) in enumerate(A_PARTS):
                rs2a[k, q] = send(ea.at[half[h], zs, yhl(p)[0], gs], ry2.at[y, zs, gs], to)
            rsu["y2", k] = send(u2.at[h], u2y.at[y], to)

    second_a(0)
    second_a(1)
    top = jnp.full((8, 128), LEAST, F32)
    for k in range(1, Y):
        got(rsu["y", k], uy.at[at_y(-k)[0]])
    for q, (zs, gs, ls) in enumerate(B_PARTS):
        total = gall[c, yl, zs, yh, :, gs]
        for k in range(1, Y):
            src = at_y(-k)[0]
            got(rsb[k, q], ry1.at[src, zs, :, ls])
            total = total + decode(ry1[src, zs, :, ls], uy[src])
        sb[zs, :, ls] = total
        top = jnp.maximum(top, largest(total))
    u2[2] = top * (1.0 / TOP)
    for zs, gs, ls in B_PARTS:
        eb[zs, :, ls] = encode(sb[zs, :, ls], TOP / top)
    for k in range(1, X):
        p, to = at_x(k)
        for q, (zs, gs, ls) in enumerate(B_PARTS):
            rs2b[k, q] = send(eb.at[zs, p, ls], rx2.at[x, zs, ls], to)
        rsu["x2", k] = send(u2.at[2], u2x.at[x], to)
    for k in range(1, Z):
        for h in range(2):
            got(rsz[k, h], rz1.at[at_z(-k)[0], half[h]], even)
            got(rsu["z", k, h], uz.at[at_z(-k)[0], half[h]], even)

    @pl.when(even)
    def _():
        for w in range(2):
            total = gall[c, w, pz, :, :, G3]
            for k in range(1, Z):
                src = at_z(-k)[0]
                total = total + decode(rz1[src, w], uz[src, w])
            sc[w] = total

    for k in range(1, X):
        p, to = at_x(k)
        rsc2[k] = send(sc.at[:, :, p], rc2.at[x], to, even)

    a_slab = lambda p, q, cc: wb.at[:, A_PARTS[q][0], cc, :, p, A_PARTS[q][1]]
    b_slab = lambda p, q, cc: wb.at[yhl(p)[1], B_PARTS[q][0], cc, yhl(p)[0], :, B_PARTS[q][1]]
    relay_a, relay_b = {}, {}

    def relay(ref):
        return send(ref, ref, sibling)

    for q in range(2):
        relay_a[0, q] = relay(a_slab(x, q, c))
    for q in range(3):
        relay_b[0, q] = relay(b_slab(y, q, c))
    for k in range(1, X):
        for q in range(2):
            for m in range(Y):
                got(ag3a[k, q, m], a_piece(at_y(-m)[0], at_x(-k)[0], q))
            relay_a[k, q] = relay(a_slab(at_x(-k)[0], q, c))
        for q in range(3):
            for m in range(X):
                got(ag3b[k, q, m], b_piece(at_y(-k)[0], at_x(-m)[0], q))
            relay_b[k, q] = relay(b_slab(at_y(-k)[0], q, c))
    for k in range(1, Z):
        got(ag3c[k], c_slab(at_z(-k)[0]), away(k)[0])
    c_all = lambda cc: wb.at[:, C_PLACES, cc, :, :, G3]
    relay_c = relay(c_all(c))

    for k in range(1, X):
        got(bias_x[k - 1], bx.at[at_x(-k)[0]])
    by[y] = (bx[0] + bx[1]) + (bx[2] + bx[3])
    bias_y = [send(by.at[y], by.at[y], at_y(k)[1]) for k in range(1, Y)]

    for k in range(1, Y):
        got(rsu["y2", k], u2y.at[at_y(-k)[0]])
    for q, (zs, gs) in enumerate(A_PARTS):
        total = sa[yl, zs, yh, gs]
        for k in range(1, Y):
            src = at_y(-k)[0]
            got(rs2a[k, q], ry2.at[src, zs, gs])
            total = total + decode(ry2[src, zs, gs], u2y[src])
        s2[zs, gs] = total
    for k in range(1, X):
        got(rsu["x2", k], u2x.at[at_x(-k)[0]])
    for q, (zs, gs, ls) in enumerate(B_PARTS):
        total = sb[zs, x, ls]
        for k in range(1, X):
            src = at_x(-k)[0]
            got(rs2b[k, q], rx2.at[src, zs, ls])
            total = total + decode(rx2[src, zs, ls], u2x[src])
        s2[zs, gs] = total
    rs3, rs3o, rsc3 = {}, {}, {}
    first3 = pl.ds(0, 3)
    for k in range(1, Z):
        p, to = at_z(k)
        place = reversed_bits(p)
        rs3[k] = send(s2.at[place, first3], rz3.at[z, first3], to)
        rs3o[k] = send(s2.at[place, G3], rz3.at[z, G3], to, away(k)[1])
    for k in range(1, X):
        got(rsc2[k], rc2.at[at_x(-k)[0]], even)

    @pl.when(even)
    def _():
        total = sc[:, :, x]
        for k in range(1, X):
            total = total + rc2[at_x(-k)[0]]
        sc2[...] = total

    for k in range(1, Y):
        p, to = at_y(k)
        ph, pw = yhl(p)
        rsc3[k] = send(sc2.at[pw, ph], rc3.at[y], to, even)
    for k in range(X):
        for q in range(2):
            got(relay_a[k, q], a_slab(at_x(-k)[0], q, 1 - c))
        for q in range(3):
            got(relay_b[k, q], b_slab(at_y(-k)[0], q, 1 - c))
    got(relay_c, c_all(1 - c))
    acc[...] = jnp.broadcast_to(bias_ref[...], acc.shape)

    def products(lo, hi):
        @pl.loop(lo, hi)
        def _(j):
            q = lax.rem(j, 4)
            p = lax.rem(q, 2) * 2 + q // 2
            w = jnp.concatenate(
                [
                    jnp.concatenate(
                        [wb[j // 4, p + d, :, :, :, g].reshape(256, 128) for d in (0, 4)], axis=0
                    )
                    for g in range(4)
                ],
                axis=1,
            )
            cols = pl.ds(pl.multiple_of(j * 512, 512), 512)
            gto[:, cols] = lax.dot_general(
                gv[...], w, (((1,), (1,)), ((), ())), preferred_element_type=F32
            ).astype(BF16)
            acc[...] += jnp.dot(tok[:, cols], w, preferred_element_type=F32)

    products(0, 4)

    for k in range(1, Y):
        got(bias_y[k - 1], by.at[at_y(-k)[0]])
    bz[z] = (by[0] + by[1]) + (by[2] + by[3])
    bias_z = [send(bz.at[z], bz.at[z], at_z(k)[1]) for k in range(1, Z)]
    products(4, 8)
    valo[...] = acc[...].astype(BF16)

    for k in range(1, Z):
        got(bias_z[k - 1], bz.at[at_z(-k)[0]])
    total = bz[0]
    for k in range(1, Z):
        total = total + bz[k]
    gb_ref[...] = jnp.sum(total, axis=0, keepdims=True) * scale
    for k in range(1, Y):
        got(rsc3[k], rc3.at[at_y(-k)[0]], even)

    @pl.when(even)
    def _():
        total = sc2[yl, yh, 0]
        for k in range(1, Y):
            total = total + rc3[at_y(-k)[0], 0]
        gw_ref[:, pl.ds(384, 128)] = total

    for k in range(1, Z):
        got(rs3[k], rz3.at[at_z(-k)[0], first3])
        got(rs3o[k], rz3.at[at_z(-k)[0], G3], odd)
    total = s2[pz, first3]
    for k in range(1, Z):
        total = total + rz3[at_z(-k)[0], first3]
    for g in range(3):
        gw_ref[:, pl.ds(g * 128, 128)] = total[g]

    @pl.when(odd)
    def _():
        total = s2[pz, 3]
        for k in range(1, Z):
            total = total + rz3[at_z(-k)[0], 3]
        gw_ref[:, pl.ds(384, 128)] = total

    for cp_, when in sends:
        only(when, lambda: cp_.wait_send())

    @pl.loop(0, 2 * Z)
    def _(i):
        pltpu.make_async_remote_copy(
            src_ref=gr.at[0, 0], dst_ref=gr.at[0, 0], send_sem=dsem.at[i], recv_sem=drsem.at[i],
            device_id=sibling, device_id_type=MESH,
        ).wait_send()
    assert count[0] <= N_SEM, count[0]


def write_kernel(val, gt, gw, gb, val_out, gt_out, gw_out, gb_out, sem):
    copies = [pltpu.make_async_copy(val, val_out, sem.at[0])]
    rows = gt.shape[0] // 4
    for q in range(4):
        part = pl.ds(q * rows, rows)
        copies.append(pltpu.make_async_copy(gt.at[part], gt_out.at[part], sem.at[1 + q]))
    copies.append(pltpu.make_async_copy(gw, gw_out, sem.at[5]))
    copies.append(pltpu.make_async_copy(gb, gb_out, sem.at[6]))
    for cp_ in copies:
        cp_.start()
    for cp_ in copies:
        cp_.wait()


def shards(tokens, weight, bias, grad_values):
    rows, width = tokens.shape
    feats = weight.shape[1]
    n = lax.axis_size("outer") * lax.axis_size("inner")
    scale = float(1.0 / (rows * n) ** 0.5)
    anyspace = pl.BlockSpec(memory_space=pl.ANY)
    vmem = pl.BlockSpec(memory_space=pltpu.VMEM)
    tile = (16, 128)
    scratch = [
        ((rows, width), BF16),
        ((rows, feats), BF16),
        ((2, Z, 2, 2, X, 4) + tile, BF16),
        ((2, 2, Z, 2, X, 4) + tile, F32),
        ((2, Z, 2, X, 4) + tile, F32),
        ((rows, feats), F32),
        ((X, 2, Z, 2, 2) + tile, BF16),
        ((Y, Z, X, 3) + tile, BF16),
        ((Z, 2, 2, X, 1) + tile, BF16),
        ((2, Z, 2, 2) + tile, F32),
        ((Z, X, 3) + tile, F32),
        ((2, 2, X, 1) + tile, F32),
        ((Y, Z, 2) + tile, BF16),
        ((X, Z, 3) + tile, BF16),
        ((X, 2, 2, 1) + tile, F32),
        ((Z, 4) + tile, F32),
        ((2, 2, 1) + tile, F32),
        ((Z, 4) + tile, F32),
        ((Y, 1) + tile, F32),
        ((2, Z, 2, X, 4) + tile, BF16),
        ((2, Z, 2, 2) + tile, BF16),
        ((Z, X, 3) + tile, BF16),
        ((2, 8, 128), F32),
        ((X, 2, 8, 128), F32),
        ((Y, 8, 128), F32),
        ((Z, 2, 8, 128), F32),
        ((3, 8, 128), F32),
        ((Y, 8, 128), F32),
        ((X, 8, 128), F32),
        ((2, 8, feats), F32),
        ((X, 8, feats), F32),
        ((Y, 8, feats), F32),
        ((Z, 8, feats), F32),
    ]
    dma = pltpu.SemaphoreType.DMA
    outs = (
        ((rows, feats), BF16),
        ((rows, width), BF16),
        (weight.shape, F32),
        ((1, feats), F32),
    )
    results = pl.pallas_call(
        functools.partial(kernel, scale),
        out_shape=tuple(pltpu.VMEM(s, d) for s, d in outs),
        in_specs=[anyspace, anyspace, vmem, anyspace],
        out_specs=(vmem,) * 4,
        scratch_shapes=[pltpu.VMEM(s, d) for s, d in scratch]
        + [dma((N_SEM,)), dma((N_SEM,)), dma((2 * Z,)), dma((2 * Z,)), dma((8,))],
        compiler_params=pltpu.CompilerParams(
            collective_id=0, has_side_effects=True, vmem_limit_bytes=50 * 1024 * 1024
        ),
        cost_estimate=pl.CostEstimate(
            flops=6 * rows * width * feats, bytes_accessed=4 * rows * width, transcendentals=0
        ),
        name="gather_scatter",
    )(tokens, weight, bias.reshape(1, feats), grad_values)
    values, grad_tokens, grad_weight, grad_bias = pl.pallas_call(
        write_kernel,
        out_shape=tuple(jax.ShapeDtypeStruct(s, d) for s, d in outs),
        in_specs=[vmem] * 4,
        out_specs=(anyspace,) * 4,
        scratch_shapes=[dma((8,))],
        compiler_params=pltpu.CompilerParams(vmem_limit_bytes=1024 * 1024),
        name="write",
    )(*[pltpu.with_memory_space_constraint(r, pltpu.VMEM) for r in results])
    return values, grad_tokens, grad_weight, grad_bias.reshape(feats)


def solution(mesh):
    in_specs = (
        P(("outer", "inner"), None),
        P(("outer", "inner"), None),
        P(),
        P(("outer", "inner"), None),
    )
    out_specs = (
        P(("outer", "inner"), None),
        P(("outer", "inner"), None),
        P(("outer", "inner"), None),
        P(),
    )
    return jax.shard_map(shards, mesh=mesh, in_specs=in_specs, out_specs=out_specs, check_vma=False)
```

```python
import functools

import jax
import jax.numpy as jnp
from jax import lax
from jax.experimental import pallas as pl
from jax.experimental.pallas import tpu as pltpu
from jax.sharding import PartitionSpec as P

X, Y, Z = 4, 4, 8
MESH = pl.DeviceIdType.MESH
F32, BF16 = jnp.float32, jnp.bfloat16
N_SEM = 260
A_PARTS = ((pl.ds(0, 6), pl.ds(0, 2)), (pl.ds(6, 2), pl.ds(0, 1)))
B_PARTS = (
    (pl.ds(0, 4), pl.ds(2, 1), pl.ds(1, 1)),
    (pl.ds(4, 2), pl.ds(2, 2), pl.ds(1, 2)),
    (pl.ds(6, 2), pl.ds(1, 3), pl.ds(0, 3)),
)
C_PLACES = pl.ds(0, 4)
G3 = pl.ds(3, 1)


TOP = 2.0 ** 15.5
LEAST = 2.0 ** -100
NORMAL = 2.0 ** -126


def tiles(v):
    return v.reshape(v.shape[:-2] + (2, 8, 128))


def largest(v):
    return jnp.max(jnp.abs(v).reshape(-1, 8, 128), axis=0)


def encode(v, inverse):
    r = (tiles(v) * inverse).reshape(v.shape)
    r2 = r * r
    r4 = r2 * r2
    r8 = r4 * r4
    return jnp.where(r < 0, -r8, r8).astype(BF16)


def decode(code, unit):
    v = code.astype(F32)
    r2 = lax.rsqrt(jnp.maximum(jnp.abs(v), NORMAL))
    r4 = lax.rsqrt(r2)
    root = r4 * lax.rsqrt(r4)
    return (tiles(jnp.where(v < 0, -root, root)) * unit).reshape(v.shape)


def reversed_bits(i):
    return lax.rem(i, 2) * 4 + lax.rem(i // 2, 2) * 2 + i // 4


def kernel(
    scale,
    tok_hbm, w_hbm, bias_ref, gv_hbm,
    valo, gto, gw_ref, gb_ref,
    tok, gv, wb, gall, gr, acc,
    rx1, ry1, rz1, sa, sb, sc, ry2, rx2, rc2, s2, sc2, rz3, rc3,
    code, ea, eb, u, ux, uy, uz, u2, u2y, u2x,
    bb, bx, by, bz,
    ssem, rsem, dsem, drsem, lsem,
):
    outer = lax.axis_index("outer")
    inner = lax.axis_index("inner")
    c = lax.rem(outer, 2)
    z = lax.rem(outer // 2, Z)
    yl = outer // (2 * Z)
    x = lax.rem(inner, X)
    yh = inner // X
    y = yh * 2 + yl
    pz = reversed_bits(z)
    even = lax.rem(z, 2) == 0
    odd = lax.rem(z, 2) == 1

    def dev(px, py, pz_, pc):
        return {
            "outer": (lax.rem(py, 2) * Z + pz_) * 2 + pc,
            "inner": (py // 2) * X + px,
        }

    def at_x(k):
        p = lax.rem(x + k + X, X)
        return p, dev(p, y, z, c)

    def at_y(k):
        p = lax.rem(y + k + Y, Y)
        return p, dev(x, p, z, c)

    def at_z(k):
        p = lax.rem(z + k + Z, Z)
        return p, dev(x, y, p, c)

    def away(k):
        return (even, odd) if k % 2 == 0 else (odd, even)

    sibling = dev(x, y, z, 1 - c)
    yhl = lambda p: (p // 2, lax.rem(p, 2))
    count = [0]
    sends = []

    def only(when, act):
        if when is None:
            act()
        else:
            pl.when(when)(act)

    def send(src, dst, to, when=None):
        i = count[0]
        count[0] += 1
        cp_ = pltpu.make_async_remote_copy(
            src_ref=src, dst_ref=dst, send_sem=ssem.at[i], recv_sem=rsem.at[i],
            device_id=to, device_id_type=MESH,
        )
        only(when, lambda: cp_.start())
        sends.append((cp_, when))
        return i

    def got(i, dst, when=None):
        cp_ = pltpu.make_async_remote_copy(
            src_ref=dst, dst_ref=dst, send_sem=ssem.at[i], recv_sem=rsem.at[i],
            device_id=sibling, device_id_type=MESH,
        )
        only(when, lambda: cp_.wait_recv())

    half = (1 - yl, yl)
    tok_in = []
    for h in range(2):
        cols = pl.ds(pl.multiple_of(half[h] * 2048, 2048), 2048)
        tok_in.append(pltpu.make_async_copy(tok_hbm.at[:, cols], tok.at[:, cols], lsem.at[h]))
    gv_in = pltpu.make_async_copy(gv_hbm, gv, lsem.at[2])
    w_in = [
        pltpu.make_async_copy(
            w_hbm.at[:, pl.ds(g * 128, 128)], wb.at[yl, pz, c, yh, x, g], lsem.at[3 + g]
        )
        for g in range(4)
    ]
    for cp_ in w_in:
        cp_.start()
    barrier = pltpu.get_barrier_semaphore()
    peers = [at_z(k)[1] for k in range(1, Z)] + [at_x(k)[1] for k in range(1, X)]
    peers += [at_y(k)[1] for k in range(1, Y)] + [sibling]
    for p in peers:
        pl.semaphore_signal(barrier, inc=1, device_id=p, device_id_type=MESH)
    gv_in.start()
    tok_in[0].start()
    tok_in[1].start()

    def d2d(h, i):
        return pltpu.make_async_remote_copy(
            src_ref=gall.at[1 - c, half[h], i], dst_ref=gr.at[half[h], i],
            send_sem=dsem.at[h * Z + i], recv_sem=drsem.at[h * Z + i],
            device_id=sibling, device_id_type=MESH,
        )

    def grads(h, lo, hi):
        @pl.loop(lo, hi)
        def _(i):
            col = pl.multiple_of((half[h] * Z + reversed_bits(i)) * 256, 256)
            part = lax.dot_general(
                tok[:, pl.ds(col, 256)], gv[...], (((0,), (0,)), ((), ())),
                preferred_element_type=F32,
            ) * scale
            for g in range(4):
                gall[:, half[h], i, :, :, g] = part[:, g * 128:(g + 1) * 128].reshape(
                    2, 2, X, 16, 128
                )
            d2d(h, i).start()

    for cp_ in w_in:
        cp_.wait()
    pl.semaphore_wait(barrier, len(peers))

    own = lambda gs: wb.at[yl, pz, c, yh, x, gs]
    ag1, ag1o, agc1 = {}, {}, {}
    for k in range(1, Z):
        to = at_z(k)[1]
        ag1[k] = send(own(pl.ds(0, 3)), own(pl.ds(0, 3)), to)
        ag1o[k] = send(own(G3), own(G3), to, odd)
    for k in range(1, Y):
        agc1[k] = send(own(G3), own(G3), at_y(k)[1], even)

    gv_in.wait()
    tok_in[0].wait()
    grads(0, 0, Z)
    tok_in[1].wait()
    grads(1, 0, 4)

    def combine(h):
        def add(i, top):
            pltpu.make_async_remote_copy(
                src_ref=gr.at[half[h], i], dst_ref=gr.at[half[h], i],
                send_sem=dsem.at[h * Z + i], recv_sem=drsem.at[h * Z + i],
                device_id=sibling, device_id_type=MESH,
            ).wait_recv()
            both = gall[c, half[h], i] + gr[half[h], i]
            gall[c, half[h], i] = both
            return jnp.maximum(top, largest(both))

        top = lax.fori_loop(0, Z, add, jnp.full((8, 128), LEAST, F32))
        u[h] = top * (1.0 / TOP)
        inverse = TOP / top

        @pl.loop(0, Z)
        def _(i):
            code[half[h], i] = encode(gall[c, half[h], i], inverse)

    rsa, rsb, rsz, rsu = {}, {}, {}, {}

    def scatter_first(h):
        for k in range(1, X):
            p, to = at_x(k)
            for q, (zs, gs) in enumerate(A_PARTS):
                rsa[k, q, h] = send(
                    code.at[half[h], zs, :, p, gs], rx1.at[x, half[h], zs, :, gs], to
                )
            rsu["x", k, h] = send(u.at[h], ux.at[x, h], to)
        for k in ((1, 3), (2,))[h]:
            p, to = at_y(k)
            for q, (zs, gs, ls) in enumerate(B_PARTS):
                rsb[k, q] = send(
                    code.at[half[h], zs, yhl(p)[0], :, gs], ry1.at[y, zs, :, ls], to
                )
            rsu["y", k] = send(u.at[h], uy.at[y], to)
        for k in range(1, Z):
            p, to = at_z(k)
            rsz[k, h] = send(
                code.at[half[h], reversed_bits(p), :, :, G3], rz1.at[z, half[h]], to, away(k)[0]
            )
            rsu["z", k, h] = send(u.at[h], uz.at[z, half[h]], to, away(k)[0])

    combine(0)
    scatter_first(0)

    for k in range(1, Z):
        place = reversed_bits(at_z(-k)[0])
        got(ag1[k], wb.at[yl, place, c, yh, x, pl.ds(0, 3)])
        got(ag1o[k], wb.at[yl, place, c, yh, x, G3], away(k)[1])
    a_piece = lambda py, px, q: wb.at[
        yhl(py)[1], A_PARTS[q][0], c, yhl(py)[0], px, A_PARTS[q][1]
    ]
    b_piece = lambda py, px, q: wb.at[
        yhl(py)[1], B_PARTS[q][0], c, yhl(py)[0], px, B_PARTS[q][1]
    ]
    ag2a, ag2b, agc2, ag3a, ag3b, ag3c = {}, {}, {}, {}, {}, {}
    for k in range(1, Y):
        for q in range(2):
            ref = a_piece(y, x, q)
            ag2a[k, q] = send(ref, ref, at_y(k)[1])
    for k in range(1, X):
        for q in range(3):
            ref = b_piece(y, x, q)
            ag2b[k, q] = send(ref, ref, at_x(k)[1])
    for k in range(1, Y):
        ph, pw = yhl(at_y(-k)[0])
        got(agc1[k], wb.at[pw, pz, c, ph, x, G3], even)
    for k in range(1, X):
        ref = wb.at[:, pz, c, :, x, G3]
        agc2[k] = send(ref, ref, at_x(k)[1], even)

    def spread_a(m, ks):
        for k in ks:
            for q in range(2):
                ref = a_piece(at_y(-m)[0], x, q)
                ag3a[k, q, m] = send(ref, ref, at_x(k)[1])

    def spread_b(m, ks):
        for k in ks:
            for q in range(3):
                ref = b_piece(y, at_x(-m)[0], q)
                ag3b[k, q, m] = send(ref, ref, at_y(k)[1])

    spread_a(0, (1, 3, 2))
    spread_b(0, (1, 3, 2))

    grads(1, 4, Z)
    gvf = gv[...].astype(F32)
    bb[c] = jnp.sum(gvf.reshape(-1, 8, 512), axis=0)
    bias_core = send(bb.at[c], bb.at[c], sibling)

    for k in range(1, X):
        got(agc2[k], wb.at[:, pz, c, :, at_x(-k)[0], G3], even)
    c_slab = lambda p: wb.at[:, reversed_bits(p), c, :, :, G3]
    for k in range(1, Z):
        ag3c[k] = send(c_slab(z), c_slab(z), at_z(k)[1], even)

    combine(1)
    scatter_first(1)

    for m in range(1, X):
        for q in range(2):
            got(ag2a[m, q], a_piece(at_y(-m)[0], x, q))
        spread_a(m, (1, 3))
        for q in range(3):
            got(ag2b[m, q], b_piece(y, at_x(-m)[0], q))
        spread_b(m, (1, 3))

    got(bias_core, bb.at[1 - c])
    bx[x] = bb[0] + bb[1]
    bias_x = [send(bx.at[x], bx.at[x], at_x(k)[1]) for k in range(1, X)]

    rs2a, rs2b, rsc2 = {}, {}, {}

    def second_a(h):
        top = jnp.full((8, 128), LEAST, F32)
        for k in range(1, X):
            got(rsu["x", k, h], ux.at[at_x(-k)[0], h])
        for q, (zs, gs) in enumerate(A_PARTS):
            total = gall[c, half[h], zs, :, x, gs]
            for k in range(1, X):
                src = at_x(-k)[0]
                got(rsa[k, q, h], rx1.at[src, half[h], zs, :, gs])
                total = total + decode(rx1[src, half[h], zs, :, gs], ux[src, h])
            sa[half[h], zs, :, gs] = total
            top = jnp.maximum(top, largest(total))
        u2[h] = top * (1.0 / TOP)
        for zs, gs in A_PARTS:
            ea[half[h], zs, :, gs] = encode(sa[half[h], zs, :, gs], TOP / top)
        for k in ((1, 3), (2,))[h]:
            p, to = at_y(k)
            for q, (zs, gs) in enumerate(A_PARTS):
                rs2a[k, q] = send(ea.at[half[h], zs, yhl(p)[0], gs], ry2.at[y, zs, gs], to)
            rsu["y2", k] = send(u2.at[h], u2y.at[y], to)

    second_a(0)
    second_a(1)
    for m in range(1, X):
        spread_a(m, (2,))
        spread_b(m, (2,))
    top = jnp.full((8, 128), LEAST, F32)
    for k in range(1, Y):
        got(rsu["y", k], uy.at[at_y(-k)[0]])
    for q, (zs, gs, ls) in enumerate(B_PARTS):
        total = gall[c, yl, zs, yh, :, gs]
        for k in range(1, Y):
            src = at_y(-k)[0]
            got(rsb[k, q], ry1.at[src, zs, :, ls])
            total = total + decode(ry1[src, zs, :, ls], uy[src])
        sb[zs, :, ls] = total
        top = jnp.maximum(top, largest(total))
    u2[2] = top * (1.0 / TOP)
    for zs, gs, ls in B_PARTS:
        eb[zs, :, ls] = encode(sb[zs, :, ls], TOP / top)
    for k in range(1, X):
        p, to = at_x(k)
        for q, (zs, gs, ls) in enumerate(B_PARTS):
            rs2b[k, q] = send(eb.at[zs, p, ls], rx2.at[x, zs, ls], to)
        rsu["x2", k] = send(u2.at[2], u2x.at[x], to)
    for k in range(1, Z):
        for h in range(2):
            got(rsz[k, h], rz1.at[at_z(-k)[0], half[h]], even)
            got(rsu["z", k, h], uz.at[at_z(-k)[0], half[h]], even)

    @pl.when(even)
    def _():
        for w in range(2):
            total = gall[c, w, pz, :, :, G3]
            for k in range(1, Z):
                src = at_z(-k)[0]
                total = total + decode(rz1[src, w], uz[src, w])
            sc[w] = total

    for k in range(1, X):
        p, to = at_x(k)
        rsc2[k] = send(sc.at[:, :, p], rc2.at[x], to, even)

    a_slab = lambda p, q, cc: wb.at[:, A_PARTS[q][0], cc, :, p, A_PARTS[q][1]]
    b_slab = lambda p, q, cc: wb.at[yhl(p)[1], B_PARTS[q][0], cc, yhl(p)[0], :, B_PARTS[q][1]]
    relay_a, relay_b = {}, {}

    def relay(ref):
        return send(ref, ref, sibling)

    for q in range(2):
        relay_a[0, q] = relay(a_slab(x, q, c))
    for q in range(3):
        relay_b[0, q] = relay(b_slab(y, q, c))
    for k in (1, 3, 2):
        for q in range(2):
            for m in range(Y):
                got(ag3a[k, q, m], a_piece(at_y(-m)[0], at_x(-k)[0], q))
            relay_a[k, q] = relay(a_slab(at_x(-k)[0], q, c))
        for q in range(3):
            for m in range(X):
                got(ag3b[k, q, m], b_piece(at_y(-k)[0], at_x(-m)[0], q))
            relay_b[k, q] = relay(b_slab(at_y(-k)[0], q, c))
    for k in range(1, Z):
        got(ag3c[k], c_slab(at_z(-k)[0]), away(k)[0])
    c_all = lambda cc: wb.at[:, C_PLACES, cc, :, :, G3]
    relay_c = relay(c_all(c))

    for k in range(1, X):
        got(bias_x[k - 1], bx.at[at_x(-k)[0]])
    by[y] = (bx[0] + bx[1]) + (bx[2] + bx[3])
    bias_y = [send(by.at[y], by.at[y], at_y(k)[1]) for k in range(1, Y)]

    for k in range(1, Y):
        got(rsu["y2", k], u2y.at[at_y(-k)[0]])
    for q, (zs, gs) in enumerate(A_PARTS):
        total = sa[yl, zs, yh, gs]
        for k in range(1, Y):
            src = at_y(-k)[0]
            got(rs2a[k, q], ry2.at[src, zs, gs])
            total = total + decode(ry2[src, zs, gs], u2y[src])
        s2[zs, gs] = total
    for k in range(1, X):
        got(rsu["x2", k], u2x.at[at_x(-k)[0]])
    for q, (zs, gs, ls) in enumerate(B_PARTS):
        total = sb[zs, x, ls]
        for k in range(1, X):
            src = at_x(-k)[0]
            got(rs2b[k, q], rx2.at[src, zs, ls])
            total = total + decode(rx2[src, zs, ls], u2x[src])
        s2[zs, gs] = total
    rs3, rs3o, rsc3 = {}, {}, {}
    first3 = pl.ds(0, 3)
    for k in range(1, Z):
        p, to = at_z(k)
        place = reversed_bits(p)
        rs3[k] = send(s2.at[place, first3], rz3.at[z, first3], to)
        rs3o[k] = send(s2.at[place, G3], rz3.at[z, G3], to, away(k)[1])
    for k in range(1, X):
        got(rsc2[k], rc2.at[at_x(-k)[0]], even)

    @pl.when(even)
    def _():
        total = sc[:, :, x]
        for k in range(1, X):
            total = total + rc2[at_x(-k)[0]]
        sc2[...] = total

    for k in range(1, Y):
        p, to = at_y(k)
        ph, pw = yhl(p)
        rsc3[k] = send(sc2.at[pw, ph], rc3.at[y], to, even)
    for k in range(X):
        for q in range(2):
            got(relay_a[k, q], a_slab(at_x(-k)[0], q, 1 - c))
        for q in range(3):
            got(relay_b[k, q], b_slab(at_y(-k)[0], q, 1 - c))
    got(relay_c, c_all(1 - c))
    acc[...] = jnp.broadcast_to(bias_ref[...], acc.shape)

    def products(lo, hi):
        @pl.loop(lo, hi)
        def _(j):
            q = lax.rem(j, 4)
            p = lax.rem(q, 2) * 2 + q // 2
            w = jnp.concatenate(
                [
                    jnp.concatenate(
                        [wb[j // 4, p + d, :, :, :, g].reshape(256, 128) for d in (0, 4)], axis=0
                    )
                    for g in range(4)
                ],
                axis=1,
            )
            cols = pl.ds(pl.multiple_of(j * 512, 512), 512)
            gto[:, cols] = lax.dot_general(
                gv[...], w, (((1,), (1,)), ((), ())), preferred_element_type=F32
            ).astype(BF16)
            acc[...] += jnp.dot(tok[:, cols], w, preferred_element_type=F32)

    products(0, 4)

    for k in range(1, Y):
        got(bias_y[k - 1], by.at[at_y(-k)[0]])
    bz[z] = (by[0] + by[1]) + (by[2] + by[3])
    bias_z = [send(bz.at[z], bz.at[z], at_z(k)[1]) for k in range(1, Z)]
    products(4, 8)
    valo[...] = acc[...].astype(BF16)

    for k in range(1, Z):
        got(bias_z[k - 1], bz.at[at_z(-k)[0]])
    total = bz[0]
    for k in range(1, Z):
        total = total + bz[k]
    gb_ref[...] = jnp.sum(total, axis=0, keepdims=True) * scale
    for k in range(1, Y):
        got(rsc3[k], rc3.at[at_y(-k)[0]], even)

    @pl.when(even)
    def _():
        total = sc2[yl, yh, 0]
        for k in range(1, Y):
            total = total + rc3[at_y(-k)[0], 0]
        gw_ref[:, pl.ds(384, 128)] = total

    for k in range(1, Z):
        got(rs3[k], rz3.at[at_z(-k)[0], first3])
        got(rs3o[k], rz3.at[at_z(-k)[0], G3], odd)
    total = s2[pz, first3]
    for k in range(1, Z):
        total = total + rz3[at_z(-k)[0], first3]
    for g in range(3):
        gw_ref[:, pl.ds(g * 128, 128)] = total[g]

    @pl.when(odd)
    def _():
        total = s2[pz, 3]
        for k in range(1, Z):
            total = total + rz3[at_z(-k)[0], 3]
        gw_ref[:, pl.ds(384, 128)] = total

    for cp_, when in sends:
        only(when, lambda: cp_.wait_send())

    @pl.loop(0, 2 * Z)
    def _(i):
        pltpu.make_async_remote_copy(
            src_ref=gr.at[0, 0], dst_ref=gr.at[0, 0], send_sem=dsem.at[i], recv_sem=drsem.at[i],
            device_id=sibling, device_id_type=MESH,
        ).wait_send()
    assert count[0] <= N_SEM, count[0]


def write_kernel(val, gt, gw, gb, val_out, gt_out, gw_out, gb_out, sem):
    copies = [pltpu.make_async_copy(val, val_out, sem.at[0])]
    rows = gt.shape[0] // 4
    for q in range(4):
        part = pl.ds(q * rows, rows)
        copies.append(pltpu.make_async_copy(gt.at[part], gt_out.at[part], sem.at[1 + q]))
    copies.append(pltpu.make_async_copy(gw, gw_out, sem.at[5]))
    copies.append(pltpu.make_async_copy(gb, gb_out, sem.at[6]))
    for cp_ in copies:
        cp_.start()
    for cp_ in copies:
        cp_.wait()


def shards(tokens, weight, bias, grad_values):
    rows, width = tokens.shape
    feats = weight.shape[1]
    n = lax.axis_size("outer") * lax.axis_size("inner")
    scale = float(1.0 / (rows * n) ** 0.5)
    anyspace = pl.BlockSpec(memory_space=pl.ANY)
    vmem = pl.BlockSpec(memory_space=pltpu.VMEM)
    tile = (16, 128)
    scratch = [
        ((rows, width), BF16),
        ((rows, feats), BF16),
        ((2, Z, 2, 2, X, 4) + tile, BF16),
        ((2, 2, Z, 2, X, 4) + tile, F32),
        ((2, Z, 2, X, 4) + tile, F32),
        ((rows, feats), F32),
        ((X, 2, Z, 2, 2) + tile, BF16),
        ((Y, Z, X, 3) + tile, BF16),
        ((Z, 2, 2, X, 1) + tile, BF16),
        ((2, Z, 2, 2) + tile, F32),
        ((Z, X, 3) + tile, F32),
        ((2, 2, X, 1) + tile, F32),
        ((Y, Z, 2) + tile, BF16),
        ((X, Z, 3) + tile, BF16),
        ((X, 2, 2, 1) + tile, F32),
        ((Z, 4) + tile, F32),
        ((2, 2, 1) + tile, F32),
        ((Z, 4) + tile, F32),
        ((Y, 1) + tile, F32),
        ((2, Z, 2, X, 4) + tile, BF16),
        ((2, Z, 2, 2) + tile, BF16),
        ((Z, X, 3) + tile, BF16),
        ((2, 8, 128), F32),
        ((X, 2, 8, 128), F32),
        ((Y, 8, 128), F32),
        ((Z, 2, 8, 128), F32),
        ((3, 8, 128), F32),
        ((Y, 8, 128), F32),
        ((X, 8, 128), F32),
        ((2, 8, feats), F32),
        ((X, 8, feats), F32),
        ((Y, 8, feats), F32),
        ((Z, 8, feats), F32),
    ]
    dma = pltpu.SemaphoreType.DMA
    outs = (
        ((rows, feats), BF16),
        ((rows, width), BF16),
        (weight.shape, F32),
        ((1, feats), F32),
    )
    results = pl.pallas_call(
        functools.partial(kernel, scale),
        out_shape=tuple(pltpu.VMEM(s, d) for s, d in outs),
        in_specs=[anyspace, anyspace, vmem, anyspace],
        out_specs=(vmem,) * 4,
        scratch_shapes=[pltpu.VMEM(s, d) for s, d in scratch]
        + [dma((N_SEM,)), dma((N_SEM,)), dma((2 * Z,)), dma((2 * Z,)), dma((8,))],
        compiler_params=pltpu.CompilerParams(
            collective_id=0, has_side_effects=True, vmem_limit_bytes=50 * 1024 * 1024
        ),
        cost_estimate=pl.CostEstimate(
            flops=6 * rows * width * feats, bytes_accessed=4 * rows * width, transcendentals=0
        ),
        name="gather_scatter",
    )(tokens, weight, bias.reshape(1, feats), grad_values)
    values, grad_tokens, grad_weight, grad_bias = pl.pallas_call(
        write_kernel,
        out_shape=tuple(jax.ShapeDtypeStruct(s, d) for s, d in outs),
        in_specs=[vmem] * 4,
        out_specs=(anyspace,) * 4,
        scratch_shapes=[dma((8,))],
        compiler_params=pltpu.CompilerParams(vmem_limit_bytes=1024 * 1024),
        name="write",
    )(*[pltpu.with_memory_space_constraint(r, pltpu.VMEM) for r in results])
    return values, grad_tokens, grad_weight, grad_bias.reshape(feats)


def solution(mesh):
    in_specs = (
        P(("outer", "inner"), None),
        P(("outer", "inner"), None),
        P(),
        P(("outer", "inner"), None),
    )
    out_specs = (
        P(("outer", "inner"), None),
        P(("outer", "inner"), None),
        P(("outer", "inner"), None),
        P(),
    )
    return jax.shard_map(shards, mesh=mesh, in_specs=in_specs, out_specs=out_specs, check_vma=False)
```

```python
import functools

import jax
import jax.numpy as jnp
from jax import lax
from jax.experimental import pallas as pl
from jax.experimental.pallas import tpu as pltpu
from jax.sharding import PartitionSpec as P

X, Y, Z = 4, 4, 8
MESH = pl.DeviceIdType.MESH
F32, BF16 = jnp.float32, jnp.bfloat16
N_SEM = 260
A_PARTS = ((pl.ds(0, 6), pl.ds(0, 2)), (pl.ds(6, 2), pl.ds(0, 1)))
B_PARTS = (
    (pl.ds(0, 4), pl.ds(2, 1), pl.ds(1, 1)),
    (pl.ds(4, 2), pl.ds(2, 2), pl.ds(1, 2)),
    (pl.ds(6, 2), pl.ds(1, 3), pl.ds(0, 3)),
)
C_PLACES = pl.ds(0, 4)
G3 = pl.ds(3, 1)


TOP = 2.0 ** 15.5
LEAST = 2.0 ** -100
NORMAL = 2.0 ** -126


def tiles(v):
    return v.reshape(v.shape[:-2] + (2, 8, 128))


def largest(v):
    return jnp.max(jnp.abs(v).reshape(-1, 8, 128), axis=0)


def encode(v, inverse):
    r = (tiles(v) * inverse).reshape(v.shape)
    r2 = r * r
    r4 = r2 * r2
    r8 = r4 * r4
    return jnp.where(r < 0, -r8, r8).astype(BF16)


def decode(code, unit):
    v = code.astype(F32)
    r2 = lax.rsqrt(jnp.maximum(jnp.abs(v), NORMAL))
    r4 = lax.rsqrt(r2)
    root = r4 * lax.rsqrt(r4)
    return (tiles(jnp.where(v < 0, -root, root)) * unit).reshape(v.shape)


def reversed_bits(i):
    return lax.rem(i, 2) * 4 + lax.rem(i // 2, 2) * 2 + i // 4


def kernel(
    scale,
    tok_hbm, w_hbm, bias_ref, gv_hbm,
    valo, gto, gw_ref, gb_ref,
    tok, gv, wb, gall, gr, acc,
    rx1, ry1, rz1, sa, sb, sc, ry2, rx2, rc2, s2, sc2, rz3, rc3,
    code, ea, eb, u, ux, uy, uz, u2, u2y, u2x,
    bb, bx, by, bz,
    ssem, rsem, dsem, drsem, lsem,
):
    outer = lax.axis_index("outer")
    inner = lax.axis_index("inner")
    c = lax.rem(outer, 2)
    z = lax.rem(outer // 2, Z)
    yl = outer // (2 * Z)
    x = lax.rem(inner, X)
    yh = inner // X
    y = yh * 2 + yl
    pz = reversed_bits(z)
    even = lax.rem(z, 2) == 0
    odd = lax.rem(z, 2) == 1

    def dev(px, py, pz_, pc):
        return {
            "outer": (lax.rem(py, 2) * Z + pz_) * 2 + pc,
            "inner": (py // 2) * X + px,
        }

    def at_x(k):
        p = lax.rem(x + k + X, X)
        return p, dev(p, y, z, c)

    def at_y(k):
        p = lax.rem(y + k + Y, Y)
        return p, dev(x, p, z, c)

    def at_z(k):
        p = lax.rem(z + k + Z, Z)
        return p, dev(x, y, p, c)

    def away(k):
        return (even, odd) if k % 2 == 0 else (odd, even)

    sibling = dev(x, y, z, 1 - c)
    yhl = lambda p: (p // 2, lax.rem(p, 2))
    count = [0]
    sends = []

    def only(when, act):
        if when is None:
            act()
        else:
            pl.when(when)(act)

    def send(src, dst, to, when=None):
        i = count[0]
        count[0] += 1
        cp_ = pltpu.make_async_remote_copy(
            src_ref=src, dst_ref=dst, send_sem=ssem.at[i], recv_sem=rsem.at[i],
            device_id=to, device_id_type=MESH,
        )
        only(when, lambda: cp_.start())
        sends.append((cp_, when))
        return i

    def got(i, dst, when=None):
        cp_ = pltpu.make_async_remote_copy(
            src_ref=dst, dst_ref=dst, send_sem=ssem.at[i], recv_sem=rsem.at[i],
            device_id=sibling, device_id_type=MESH,
        )
        only(when, lambda: cp_.wait_recv())

    drained = [0]

    def drain(end):
        for cp_, when in sends[drained[0]:end]:
            only(when, lambda: cp_.wait_send())
        drained[0] = end

    half = (1 - yl, yl)
    tok_in = []
    for h in range(2):
        cols = pl.ds(pl.multiple_of(half[h] * 2048, 2048), 2048)
        tok_in.append(pltpu.make_async_copy(tok_hbm.at[:, cols], tok.at[:, cols], lsem.at[h]))
    gv_in = pltpu.make_async_copy(gv_hbm, gv, lsem.at[2])
    w_in = [
        pltpu.make_async_copy(
            w_hbm.at[:, pl.ds(g * 128, 128)], wb.at[yl, pz, c, yh, x, g], lsem.at[3 + g]
        )
        for g in range(4)
    ]
    for cp_ in w_in:
        cp_.start()
    barrier = pltpu.get_barrier_semaphore()
    peers = [at_z(k)[1] for k in range(1, Z)] + [at_x(k)[1] for k in range(1, X)]
    peers += [at_y(k)[1] for k in range(1, Y)] + [sibling]
    for p in peers:
        pl.semaphore_signal(barrier, inc=1, device_id=p, device_id_type=MESH)
    gv_in.start()
    tok_in[0].start()
    tok_in[1].start()

    def d2d(h, i):
        return pltpu.make_async_remote_copy(
            src_ref=gall.at[1 - c, half[h], i], dst_ref=gr.at[half[h], i],
            send_sem=dsem.at[h * Z + i], recv_sem=drsem.at[h * Z + i],
            device_id=sibling, device_id_type=MESH,
        )

    def grads(h, lo, hi):
        @pl.loop(lo, hi)
        def _(i):
            col = pl.multiple_of((half[h] * Z + reversed_bits(i)) * 256, 256)
            part = lax.dot_general(
                tok[:, pl.ds(col, 256)], gv[...], (((0,), (0,)), ((), ())),
                preferred_element_type=F32,
            ) * scale
            for g in range(4):
                gall[:, half[h], i, :, :, g] = part[:, g * 128:(g + 1) * 128].reshape(
                    2, 2, X, 16, 128
                )
            d2d(h, i).start()

    for cp_ in w_in:
        cp_.wait()
    pl.semaphore_wait(barrier, len(peers))

    own = lambda gs: wb.at[yl, pz, c, yh, x, gs]
    ag1, ag1o, agc1 = {}, {}, {}
    for k in range(1, Z):
        to = at_z(k)[1]
        ag1[k] = send(own(pl.ds(0, 3)), own(pl.ds(0, 3)), to)
        ag1o[k] = send(own(G3), own(G3), to, odd)
    for k in range(1, Y):
        agc1[k] = send(own(G3), own(G3), at_y(k)[1], even)

    gv_in.wait()
    tok_in[0].wait()
    grads(0, 0, Z)
    tok_in[1].wait()
    grads(1, 0, 4)

    def combine(h):
        def add(i, top):
            pltpu.make_async_remote_copy(
                src_ref=gr.at[half[h], i], dst_ref=gr.at[half[h], i],
                send_sem=dsem.at[h * Z + i], recv_sem=drsem.at[h * Z + i],
                device_id=sibling, device_id_type=MESH,
            ).wait_recv()
            both = gall[c, half[h], i] + gr[half[h], i]
            gall[c, half[h], i] = both
            return jnp.maximum(top, largest(both))

        top = lax.fori_loop(0, Z, add, jnp.full((8, 128), LEAST, F32))
        u[h] = top * (1.0 / TOP)
        inverse = TOP / top

        @pl.loop(0, Z)
        def _(i):
            code[half[h], i] = encode(gall[c, half[h], i], inverse)

    rsa, rsb, rsz, rsu = {}, {}, {}, {}

    def scatter_first(h):
        for k in range(1, X):
            p, to = at_x(k)
            for q, (zs, gs) in enumerate(A_PARTS):
                rsa[k, q, h] = send(
                    code.at[half[h], zs, :, p, gs], rx1.at[x, half[h], zs, :, gs], to
                )
            rsu["x", k, h] = send(u.at[h], ux.at[x, h], to)
        for k in ((1, 3), (2,))[h]:
            p, to = at_y(k)
            for q, (zs, gs, ls) in enumerate(B_PARTS):
                rsb[k, q] = send(
                    code.at[half[h], zs, yhl(p)[0], :, gs], ry1.at[y, zs, :, ls], to
                )
            rsu["y", k] = send(u.at[h], uy.at[y], to)
        for k in range(1, Z) if h == 1 else ():
            p, to = at_z(k)
            rsz[k] = send(
                code.at[:, reversed_bits(p), :, :, G3], rz1.at[z], to, away(k)[0]
            )
            rsu["z", k] = send(u, uz.at[z], to, away(k)[0])

    combine(0)
    scatter_first(0)

    for k in range(1, Z):
        place = reversed_bits(at_z(-k)[0])
        got(ag1[k], wb.at[yl, place, c, yh, x, pl.ds(0, 3)])
        got(ag1o[k], wb.at[yl, place, c, yh, x, G3], away(k)[1])
    a_piece = lambda py, px, q: wb.at[
        yhl(py)[1], A_PARTS[q][0], c, yhl(py)[0], px, A_PARTS[q][1]
    ]
    b_piece = lambda py, px, q: wb.at[
        yhl(py)[1], B_PARTS[q][0], c, yhl(py)[0], px, B_PARTS[q][1]
    ]
    ag2a, ag2b, agc2, ag3a, ag3b, ag3c = {}, {}, {}, {}, {}, {}
    for k in range(1, Y):
        for q in range(len(A_PARTS)):
            ref = a_piece(y, x, q)
            ag2a[k, q] = send(ref, ref, at_y(k)[1])
    for k in range(1, X):
        for q in range(len(B_PARTS)):
            ref = b_piece(y, x, q)
            ag2b[k, q] = send(ref, ref, at_x(k)[1])
    for k in range(1, Y):
        ph, pw = yhl(at_y(-k)[0])
        got(agc1[k], wb.at[pw, pz, c, ph, x, G3], even)
    for k in range(1, X):
        ref = wb.at[:, pz, c, :, x, G3]
        agc2[k] = send(ref, ref, at_x(k)[1], even)

    a_slab = lambda p, q, cc: wb.at[:, A_PARTS[q][0], cc, :, p, A_PARTS[q][1]]
    b_slab = lambda p, q, cc: wb.at[yhl(p)[1], B_PARTS[q][0], cc, yhl(p)[0], :, B_PARTS[q][1]]
    early = len(sends)

    grads(1, 4, Z)

    combine(1)
    scatter_first(1)

    for k in range(1, X):
        got(agc2[k], wb.at[:, pz, c, :, at_x(-k)[0], G3], even)
    c_slab = lambda p: wb.at[:, reversed_bits(p), c, :, :, G3]
    for k in range(1, Z):
        ag3c[k] = send(c_slab(z), c_slab(z), at_z(k)[1], even)
    for m in range(1, Y):
        for q in range(len(A_PARTS)):
            got(ag2a[m, q], a_piece(at_y(-m)[0], x, q))
    for k in range(1, X):
        for q in range(len(A_PARTS)):
            ag3a[k, q] = send(a_slab(x, q, c), a_slab(x, q, c), at_x(k)[1])
    for m in range(1, X):
        for q in range(len(B_PARTS)):
            got(ag2b[m, q], b_piece(y, at_x(-m)[0], q))
    for k in range(1, Y):
        for q in range(len(B_PARTS)):
            ag3b[k, q] = send(b_slab(y, q, c), b_slab(y, q, c), at_y(k)[1])

    bb[c] = jnp.dot(jnp.ones((8, gv.shape[0]), BF16), gv[...], preferred_element_type=F32)
    bias_core = send(bb.at[c], bb.at[c], sibling)

    rs2a, rs2b, rsc2 = {}, {}, {}

    def second_a(h):
        top = jnp.full((8, 128), LEAST, F32)
        for k in range(1, X):
            got(rsu["x", k, h], ux.at[at_x(-k)[0], h])
        for q, (zs, gs) in enumerate(A_PARTS):
            total = gall[c, half[h], zs, :, x, gs]
            for k in range(1, X):
                src = at_x(-k)[0]
                got(rsa[k, q, h], rx1.at[src, half[h], zs, :, gs])
                total = total + decode(rx1[src, half[h], zs, :, gs], ux[src, h])
            sa[half[h], zs, :, gs] = total
            top = jnp.maximum(top, largest(total))
        u2[h] = top * (1.0 / TOP)
        for zs, gs in A_PARTS:
            ea[half[h], zs, :, gs] = encode(sa[half[h], zs, :, gs], TOP / top)
        for k in ((1, 3), (2,))[h]:
            p, to = at_y(k)
            for q, (zs, gs) in enumerate(A_PARTS):
                rs2a[k, q] = send(ea.at[half[h], zs, yhl(p)[0], gs], ry2.at[y, zs, gs], to)
            rsu["y2", k] = send(u2.at[h], u2y.at[y], to)

    second_a(0)
    drain(early)
    second_a(1)
    top = jnp.full((8, 128), LEAST, F32)
    for k in range(1, Y):
        got(rsu["y", k], uy.at[at_y(-k)[0]])
    for q, (zs, gs, ls) in enumerate(B_PARTS):
        total = gall[c, yl, zs, yh, :, gs]
        for k in range(1, Y):
            src = at_y(-k)[0]
            got(rsb[k, q], ry1.at[src, zs, :, ls])
            total = total + decode(ry1[src, zs, :, ls], uy[src])
        sb[zs, :, ls] = total
        top = jnp.maximum(top, largest(total))
    u2[2] = top * (1.0 / TOP)
    for zs, gs, ls in B_PARTS:
        eb[zs, :, ls] = encode(sb[zs, :, ls], TOP / top)
    for k in range(1, X):
        p, to = at_x(k)
        for q, (zs, gs, ls) in enumerate(B_PARTS):
            rs2b[k, q] = send(eb.at[zs, p, ls], rx2.at[x, zs, ls], to)
        rsu["x2", k] = send(u2.at[2], u2x.at[x], to)
    for k in range(1, Z):
        got(rsz[k], rz1.at[at_z(-k)[0]], even)
        got(rsu["z", k], uz.at[at_z(-k)[0]], even)

    @pl.when(even)
    def _():
        for h in range(2):
            total = gall[c, half[h], pz, :, :, G3]
            for k in range(1, Z):
                src = at_z(-k)[0]
                total = total + decode(rz1[src, half[h]], uz[src, h])
            sc[half[h]] = total

    for k in range(1, X):
        p, to = at_x(k)
        rsc2[k] = send(sc.at[:, :, p], rc2.at[x], to, even)

    got(bias_core, bb.at[1 - c])
    bx[x] = bb[0] + bb[1]
    bias_x = [send(bx.at[x], bx.at[x], at_x(k)[1]) for k in range(1, X)]

    early = len(sends)

    relay_a, relay_b = {}, {}

    def relay(ref):
        return send(ref, ref, sibling)

    for q in range(len(A_PARTS)):
        relay_a[0, q] = relay(a_slab(x, q, c))
    for q in range(len(B_PARTS)):
        relay_b[0, q] = relay(b_slab(y, q, c))
    for k in (1, 3, 2):
        for q in range(len(A_PARTS)):
            got(ag3a[k, q], a_slab(at_x(-k)[0], q, c))
            relay_a[k, q] = relay(a_slab(at_x(-k)[0], q, c))
        for q in range(len(B_PARTS)):
            got(ag3b[k, q], b_slab(at_y(-k)[0], q, c))
            relay_b[k, q] = relay(b_slab(at_y(-k)[0], q, c))
    for k in range(1, Z):
        got(ag3c[k], c_slab(at_z(-k)[0]), away(k)[0])
    c_all = lambda cc: wb.at[:, C_PLACES, cc, :, :, G3]
    relay_c = relay(c_all(c))

    for k in range(1, X):
        got(bias_x[k - 1], bx.at[at_x(-k)[0]])
    by[y] = (bx[0] + bx[1]) + (bx[2] + bx[3])
    bias_y = [send(by.at[y], by.at[y], at_y(k)[1]) for k in range(1, Y)]

    drain(early)

    @pl.loop(0, 2 * Z)
    def _(i):
        pltpu.make_async_remote_copy(
            src_ref=gr.at[0, 0], dst_ref=gr.at[0, 0], send_sem=dsem.at[i], recv_sem=drsem.at[i],
            device_id=sibling, device_id_type=MESH,
        ).wait_send()

    for k in range(1, Y):
        got(rsu["y2", k], u2y.at[at_y(-k)[0]])
    for q, (zs, gs) in enumerate(A_PARTS):
        total = sa[yl, zs, yh, gs]
        for k in range(1, Y):
            src = at_y(-k)[0]
            got(rs2a[k, q], ry2.at[src, zs, gs])
            total = total + decode(ry2[src, zs, gs], u2y[src])
        s2[zs, gs] = total
    for k in range(1, X):
        got(rsu["x2", k], u2x.at[at_x(-k)[0]])
    for q, (zs, gs, ls) in enumerate(B_PARTS):
        total = sb[zs, x, ls]
        for k in range(1, X):
            src = at_x(-k)[0]
            got(rs2b[k, q], rx2.at[src, zs, ls])
            total = total + decode(rx2[src, zs, ls], u2x[src])
        s2[zs, gs] = total
    rs3, rs3o, rsc3 = {}, {}, {}
    first3 = pl.ds(0, 3)
    for k in range(1, Z):
        p, to = at_z(k)
        place = reversed_bits(p)
        rs3[k] = send(s2.at[place, first3], rz3.at[z, first3], to)
        rs3o[k] = send(s2.at[place, G3], rz3.at[z, G3], to, away(k)[1])
    for k in range(1, X):
        got(rsc2[k], rc2.at[at_x(-k)[0]], even)

    @pl.when(even)
    def _():
        total = sc[:, :, x]
        for k in range(1, X):
            total = total + rc2[at_x(-k)[0]]
        sc2[...] = total

    for k in range(1, Y):
        p, to = at_y(k)
        ph, pw = yhl(p)
        rsc3[k] = send(sc2.at[pw, ph], rc3.at[y], to, even)
    for k in range(X):
        for q in range(len(A_PARTS)):
            got(relay_a[k, q], a_slab(at_x(-k)[0], q, 1 - c))
        for q in range(len(B_PARTS)):
            got(relay_b[k, q], b_slab(at_y(-k)[0], q, 1 - c))
    got(relay_c, c_all(1 - c))
    acc[...] = jnp.broadcast_to(bias_ref[...], acc.shape)

    def products(lo, hi):
        @pl.loop(lo, hi)
        def _(j):
            q = lax.rem(j, 4)
            p = lax.rem(q, 2) * 2 + q // 2
            w = jnp.concatenate(
                [
                    jnp.concatenate(
                        [wb[j // 4, p + d, :, :, :, g].reshape(256, 128) for d in (0, 4)], axis=0
                    )
                    for g in range(4)
                ],
                axis=1,
            )
            cols = pl.ds(pl.multiple_of(j * 512, 512), 512)
            gto[:, cols] = lax.dot_general(
                gv[...], w, (((1,), (1,)), ((), ())), preferred_element_type=F32
            ).astype(BF16)
            acc[...] += jnp.dot(tok[:, cols], w, preferred_element_type=F32)

    products(0, 4)

    for k in range(1, Y):
        got(bias_y[k - 1], by.at[at_y(-k)[0]])
    bz[z] = (by[0] + by[1]) + (by[2] + by[3])
    bias_z = [send(bz.at[z], bz.at[z], at_z(k)[1]) for k in range(1, Z)]
    products(4, 8)
    valo[...] = acc[...].astype(BF16)

    for k in range(1, Z):
        got(bias_z[k - 1], bz.at[at_z(-k)[0]])
    total = bz[0]
    for k in range(1, Z):
        total = total + bz[k]
    gb_ref[...] = total[0:1] * scale
    for k in range(1, Y):
        got(rsc3[k], rc3.at[at_y(-k)[0]], even)

    @pl.when(even)
    def _():
        total = sc2[yl, yh, 0]
        for k in range(1, Y):
            total = total + rc3[at_y(-k)[0], 0]
        gw_ref[:, pl.ds(384, 128)] = total

    for k in range(1, Z):
        got(rs3[k], rz3.at[at_z(-k)[0], first3])
        got(rs3o[k], rz3.at[at_z(-k)[0], G3], odd)
    total = s2[pz, first3]
    for k in range(1, Z):
        total = total + rz3[at_z(-k)[0], first3]
    for g in range(3):
        gw_ref[:, pl.ds(g * 128, 128)] = total[g]

    @pl.when(odd)
    def _():
        total = s2[pz, 3]
        for k in range(1, Z):
            total = total + rz3[at_z(-k)[0], 3]
        gw_ref[:, pl.ds(384, 128)] = total

    drain(len(sends))
    assert count[0] <= N_SEM, count[0]


def write_kernel(val, gt, gw, gb, val_out, gt_out, gw_out, gb_out, sem):
    copies = [pltpu.make_async_copy(val, val_out, sem.at[0])]
    rows = gt.shape[0] // 4
    for q in range(4):
        part = pl.ds(q * rows, rows)
        copies.append(pltpu.make_async_copy(gt.at[part], gt_out.at[part], sem.at[1 + q]))
    copies.append(pltpu.make_async_copy(gw, gw_out, sem.at[5]))
    copies.append(pltpu.make_async_copy(gb, gb_out, sem.at[6]))
    for cp_ in copies:
        cp_.start()
    for cp_ in copies:
        cp_.wait()


def shards(tokens, weight, bias, grad_values):
    rows, width = tokens.shape
    feats = weight.shape[1]
    n = lax.axis_size("outer") * lax.axis_size("inner")
    scale = float(1.0 / (rows * n) ** 0.5)
    anyspace = pl.BlockSpec(memory_space=pl.ANY)
    vmem = pl.BlockSpec(memory_space=pltpu.VMEM)
    tile = (16, 128)
    scratch = [
        ((rows, width), BF16),
        ((rows, feats), BF16),
        ((2, Z, 2, 2, X, 4) + tile, BF16),
        ((2, 2, Z, 2, X, 4) + tile, F32),
        ((2, Z, 2, X, 4) + tile, F32),
        ((rows, feats), F32),
        ((X, 2, Z, 2, 2) + tile, BF16),
        ((Y, Z, X, 3) + tile, BF16),
        ((Z, 2, 2, X, 1) + tile, BF16),
        ((2, Z, 2, 2) + tile, F32),
        ((Z, X, 3) + tile, F32),
        ((2, 2, X, 1) + tile, F32),
        ((Y, Z, 2) + tile, BF16),
        ((X, Z, 3) + tile, BF16),
        ((X, 2, 2, 1) + tile, F32),
        ((Z, 4) + tile, F32),
        ((2, 2, 1) + tile, F32),
        ((Z, 4) + tile, F32),
        ((Y, 1) + tile, F32),
        ((2, Z, 2, X, 4) + tile, BF16),
        ((2, Z, 2, 2) + tile, BF16),
        ((Z, X, 3) + tile, BF16),
        ((2, 8, 128), F32),
        ((X, 2, 8, 128), F32),
        ((Y, 8, 128), F32),
        ((Z, 2, 8, 128), F32),
        ((3, 8, 128), F32),
        ((Y, 8, 128), F32),
        ((X, 8, 128), F32),
        ((2, 8, feats), F32),
        ((X, 8, feats), F32),
        ((Y, 8, feats), F32),
        ((Z, 8, feats), F32),
    ]
    dma = pltpu.SemaphoreType.DMA
    outs = (
        ((rows, feats), BF16),
        ((rows, width), BF16),
        (weight.shape, F32),
        ((1, feats), F32),
    )
    results = pl.pallas_call(
        functools.partial(kernel, scale),
        out_shape=tuple(pltpu.VMEM(s, d) for s, d in outs),
        in_specs=[anyspace, anyspace, vmem, anyspace],
        out_specs=(vmem,) * 4,
        scratch_shapes=[pltpu.VMEM(s, d) for s, d in scratch]
        + [dma((N_SEM,)), dma((N_SEM,)), dma((2 * Z,)), dma((2 * Z,)), dma((8,))],
        compiler_params=pltpu.CompilerParams(
            collective_id=0, has_side_effects=True, vmem_limit_bytes=50 * 1024 * 1024
        ),
        cost_estimate=pl.CostEstimate(
            flops=6 * rows * width * feats, bytes_accessed=4 * rows * width, transcendentals=0
        ),
        name="gather_scatter",
    )(tokens, weight, bias.reshape(1, feats), grad_values)
    values, grad_tokens, grad_weight, grad_bias = pl.pallas_call(
        write_kernel,
        out_shape=tuple(jax.ShapeDtypeStruct(s, d) for s, d in outs),
        in_specs=[vmem] * 4,
        out_specs=(anyspace,) * 4,
        scratch_shapes=[dma((8,))],
        compiler_params=pltpu.CompilerParams(vmem_limit_bytes=1024 * 1024),
        name="write",
    )(*[pltpu.with_memory_space_constraint(r, pltpu.VMEM) for r in results])
    return values, grad_tokens, grad_weight, grad_bias.reshape(feats)


def solution(mesh):
    in_specs = (
        P(("outer", "inner"), None),
        P(("outer", "inner"), None),
        P(),
        P(("outer", "inner"), None),
    )
    out_specs = (
        P(("outer", "inner"), None),
        P(("outer", "inner"), None),
        P(("outer", "inner"), None),
        P(),
    )
    return jax.shard_map(shards, mesh=mesh, in_specs=in_specs, out_specs=out_specs, check_vma=False)
```

```python
import functools

import jax
import jax.numpy as jnp
from jax import lax
from jax.experimental import pallas as pl
from jax.experimental.pallas import tpu as pltpu
from jax.sharding import PartitionSpec as P

X, Y, Z = 4, 4, 8
MESH = pl.DeviceIdType.MESH
F32, BF16 = jnp.float32, jnp.bfloat16
N_SEM = 260
A_PARTS = ((pl.ds(0, 6), pl.ds(0, 2)), (pl.ds(6, 2), pl.ds(0, 1)))
B_PARTS = (
    (pl.ds(0, 4), pl.ds(2, 1), pl.ds(1, 1)),
    (pl.ds(4, 2), pl.ds(2, 2), pl.ds(1, 2)),
    (pl.ds(6, 2), pl.ds(1, 3), pl.ds(0, 3)),
)
C_PLACES = pl.ds(0, 4)
G3 = pl.ds(3, 1)


TOP = 2.0 ** 15.5
LEAST = 2.0 ** -100
NORMAL = 2.0 ** -126


def tiles(v):
    return v.reshape(v.shape[:-2] + (2, 8, 128))


def largest(v):
    return jnp.max(jnp.abs(v).reshape(-1, 8, 128), axis=0)


def encode(v, inverse):
    r = (tiles(v) * inverse).reshape(v.shape)
    r2 = r * r
    r4 = r2 * r2
    r8 = r4 * r4
    return jnp.where(r < 0, -r8, r8).astype(BF16)


def decode(code, unit):
    v = code.astype(F32)
    r2 = lax.rsqrt(jnp.maximum(jnp.abs(v), NORMAL))
    r4 = lax.rsqrt(r2)
    root = r4 * lax.rsqrt(r4)
    return (tiles(jnp.where(v < 0, -root, root)) * unit).reshape(v.shape)


def reversed_bits(i):
    return lax.rem(i, 2) * 4 + lax.rem(i // 2, 2) * 2 + i // 4


def kernel(
    scale,
    tok_hbm, w_hbm, bias_ref, gv_hbm,
    valo, gto, gw_ref, gb_ref,
    tok, gv, wb, gall, gr, acc,
    rx1, ry1, rz1, sa, sb, sc, ry2, rx2, rc2, s2, sc2, rz3, rc3,
    code, ea, eb, u, ux, uy, uz, u2, u2y, u2x,
    bb, bx, by, bz,
    ssem, rsem, dsem, drsem, lsem,
):
    outer = lax.axis_index("outer")
    inner = lax.axis_index("inner")
    c = lax.rem(outer, 2)
    z = lax.rem(outer // 2, Z)
    yl = outer // (2 * Z)
    x = lax.rem(inner, X)
    yh = inner // X
    y = yh * 2 + yl
    pz = reversed_bits(z)
    even = lax.rem(z, 2) == 0
    odd = lax.rem(z, 2) == 1

    def dev(px, py, pz_, pc):
        return {
            "outer": (lax.rem(py, 2) * Z + pz_) * 2 + pc,
            "inner": (py // 2) * X + px,
        }

    def at_x(k):
        p = lax.rem(x + k + X, X)
        return p, dev(p, y, z, c)

    def at_y(k):
        p = lax.rem(y + k + Y, Y)
        return p, dev(x, p, z, c)

    def at_z(k):
        p = lax.rem(z + k + Z, Z)
        return p, dev(x, y, p, c)

    def away(k):
        return (even, odd) if k % 2 == 0 else (odd, even)

    sibling = dev(x, y, z, 1 - c)
    yhl = lambda p: (p // 2, lax.rem(p, 2))
    count = [0]
    sends = []

    def only(when, act):
        if when is None:
            act()
        else:
            pl.when(when)(act)

    def send(src, dst, to, when=None):
        i = count[0]
        count[0] += 1
        cp_ = pltpu.make_async_remote_copy(
            src_ref=src, dst_ref=dst, send_sem=ssem.at[i], recv_sem=rsem.at[i],
            device_id=to, device_id_type=MESH,
        )
        only(when, lambda: cp_.start())
        sends.append((cp_, when))
        return i

    def got(i, dst, when=None):
        cp_ = pltpu.make_async_remote_copy(
            src_ref=dst, dst_ref=dst, send_sem=ssem.at[i], recv_sem=rsem.at[i],
            device_id=sibling, device_id_type=MESH,
        )
        only(when, lambda: cp_.wait_recv())

    drained = [0]

    def drain(end):
        for cp_, when in sends[drained[0]:end]:
            only(when, lambda: cp_.wait_send())
        drained[0] = end

    half = (1 - yl, yl)
    tok_in = []
    for h in range(2):
        cols = pl.ds(pl.multiple_of(half[h] * 2048, 2048), 2048)
        tok_in.append(pltpu.make_async_copy(tok_hbm.at[:, cols], tok.at[:, cols], lsem.at[h]))
    gv_in = pltpu.make_async_copy(gv_hbm, gv, lsem.at[2])
    w_in = [
        pltpu.make_async_copy(
            w_hbm.at[:, pl.ds(g * 128, 128)], wb.at[yl, pz, c, yh, x, g], lsem.at[3 + g]
        )
        for g in range(4)
    ]
    for cp_ in w_in:
        cp_.start()
    barrier = pltpu.get_barrier_semaphore()
    peers = [at_z(k)[1] for k in range(1, Z)] + [at_x(k)[1] for k in range(1, X)]
    peers += [at_y(k)[1] for k in range(1, Y)] + [sibling]
    for p in peers:
        pl.semaphore_signal(barrier, inc=1, device_id=p, device_id_type=MESH)
    gv_in.start()
    tok_in[0].start()
    tok_in[1].start()

    def d2d(h, i):
        return pltpu.make_async_remote_copy(
            src_ref=gall.at[1 - c, half[h], i], dst_ref=gr.at[half[h], i],
            send_sem=dsem.at[h * Z + i], recv_sem=drsem.at[h * Z + i],
            device_id=sibling, device_id_type=MESH,
        )

    def grads(h, lo, hi):
        @pl.loop(lo, hi)
        def _(i):
            col = pl.multiple_of((half[h] * Z + reversed_bits(i)) * 256, 256)
            part = lax.dot_general(
                tok[:, pl.ds(col, 256)], gv[...], (((0,), (0,)), ((), ())),
                preferred_element_type=F32,
            ) * scale
            for g in range(4):
                gall[:, half[h], i, :, :, g] = part[:, g * 128:(g + 1) * 128].reshape(
                    2, 2, X, 16, 128
                )
            d2d(h, i).start()

    for cp_ in w_in:
        cp_.wait()
    pl.semaphore_wait(barrier, len(peers))

    own = lambda gs: wb.at[yl, pz, c, yh, x, gs]
    ag1, ag1o, agc1 = {}, {}, {}
    for k in range(1, Z):
        to = at_z(k)[1]
        ag1[k] = send(own(pl.ds(0, 3)), own(pl.ds(0, 3)), to)
        ag1o[k] = send(own(G3), own(G3), to, odd)
    for k in range(1, Y):
        agc1[k] = send(own(G3), own(G3), at_y(k)[1], even)

    gv_in.wait()
    tok_in[0].wait()
    grads(0, 0, Z)
    tok_in[1].wait()
    grads(1, 0, 4)

    def combine(h):
        def add(i, top):
            pltpu.make_async_remote_copy(
                src_ref=gr.at[half[h], i], dst_ref=gr.at[half[h], i],
                send_sem=dsem.at[h * Z + i], recv_sem=drsem.at[h * Z + i],
                device_id=sibling, device_id_type=MESH,
            ).wait_recv()
            both = gall[c, half[h], i] + gr[half[h], i]
            gall[c, half[h], i] = both
            return jnp.maximum(top, largest(both))

        top = lax.fori_loop(0, Z, add, jnp.full((8, 128), LEAST, F32))
        u[h] = top * (1.0 / TOP)
        inverse = TOP / top

        @pl.loop(0, Z)
        def _(i):
            code[half[h], i] = encode(gall[c, half[h], i], inverse)

    rsa, rsb, rsz, rsu = {}, {}, {}, {}

    def scatter_first(h):
        for k in range(1, X):
            p, to = at_x(k)
            for q, (zs, gs) in enumerate(A_PARTS):
                rsa[k, q, h] = send(
                    code.at[half[h], zs, :, p, gs], rx1.at[x, half[h], zs, :, gs], to
                )
            rsu["x", k, h] = send(u.at[h], ux.at[x, h], to)
        for k in ((1, 3), (2,))[h]:
            p, to = at_y(k)
            for q, (zs, gs, ls) in enumerate(B_PARTS):
                rsb[k, q] = send(
                    code.at[half[h], zs, yhl(p)[0], :, gs], ry1.at[y, zs, :, ls], to
                )
            rsu["y", k] = send(u.at[h], uy.at[y], to)
        for k in range(1, Z) if h == 1 else ():
            p, to = at_z(k)
            rsz[k] = send(
                code.at[:, reversed_bits(p), :, :, G3], rz1.at[z], to, away(k)[0]
            )
            rsu["z", k] = send(u, uz.at[z], to, away(k)[0])

    combine(0)
    scatter_first(0)

    for k in range(1, Z):
        place = reversed_bits(at_z(-k)[0])
        got(ag1[k], wb.at[yl, place, c, yh, x, pl.ds(0, 3)])
        got(ag1o[k], wb.at[yl, place, c, yh, x, G3], away(k)[1])
    a_piece = lambda py, px, q: wb.at[
        yhl(py)[1], A_PARTS[q][0], c, yhl(py)[0], px, A_PARTS[q][1]
    ]
    b_piece = lambda py, px, q: wb.at[
        yhl(py)[1], B_PARTS[q][0], c, yhl(py)[0], px, B_PARTS[q][1]
    ]
    ag2a, ag2b, agc2, ag3a, ag3b, ag3c = {}, {}, {}, {}, {}, {}
    for k in range(1, Y):
        for q in range(len(A_PARTS)):
            ref = a_piece(y, x, q)
            ag2a[k, q] = send(ref, ref, at_y(k)[1])
    for k in range(1, X):
        for q in range(len(B_PARTS)):
            ref = b_piece(y, x, q)
            ag2b[k, q] = send(ref, ref, at_x(k)[1])
    for k in range(1, Y):
        ph, pw = yhl(at_y(-k)[0])
        got(agc1[k], wb.at[pw, pz, c, ph, x, G3], even)
    for k in range(1, X):
        ref = wb.at[:, pz, c, :, x, G3]
        agc2[k] = send(ref, ref, at_x(k)[1], even)

    a_slab = lambda p, q, cc: wb.at[:, A_PARTS[q][0], cc, :, p, A_PARTS[q][1]]
    b_slab = lambda p, q, cc: wb.at[yhl(p)[1], B_PARTS[q][0], cc, yhl(p)[0], :, B_PARTS[q][1]]
    early = len(sends)

    grads(1, 4, Z)

    combine(1)
    scatter_first(1)

    for k in range(1, X):
        got(agc2[k], wb.at[:, pz, c, :, at_x(-k)[0], G3], even)
    c_slab = lambda p: wb.at[:, reversed_bits(p), c, :, :, G3]
    for k in range(1, Z):
        ag3c[k] = send(c_slab(z), c_slab(z), at_z(k)[1], even)
    for m in range(1, Y):
        for q in range(len(A_PARTS)):
            got(ag2a[m, q], a_piece(at_y(-m)[0], x, q))
    for k in range(1, X):
        for q in range(len(A_PARTS)):
            ag3a[k, q] = send(a_slab(x, q, c), a_slab(x, q, c), at_x(k)[1])
    for m in range(1, X):
        for q in range(len(B_PARTS)):
            got(ag2b[m, q], b_piece(y, at_x(-m)[0], q))
    for k in range(1, Y):
        for q in range(len(B_PARTS)):
            ag3b[k, q] = send(b_slab(y, q, c), b_slab(y, q, c), at_y(k)[1])

    bb[c] = jnp.dot(jnp.ones((8, gv.shape[0]), BF16), gv[...], preferred_element_type=F32)
    bias_core = send(bb.at[c], bb.at[c], sibling)

    rs2a, rs2b, rsc2 = {}, {}, {}

    def second_a(h):
        top = jnp.full((8, 128), LEAST, F32)
        for k in range(1, X):
            got(rsu["x", k, h], ux.at[at_x(-k)[0], h])
        for q, (zs, gs) in enumerate(A_PARTS):
            total = gall[c, half[h], zs, :, x, gs]
            for k in range(1, X):
                src = at_x(-k)[0]
                got(rsa[k, q, h], rx1.at[src, half[h], zs, :, gs])
                total = total + decode(rx1[src, half[h], zs, :, gs], ux[src, h])
            sa[half[h], zs, :, gs] = total
            top = jnp.maximum(top, largest(total))
        u2[h] = top * (1.0 / TOP)
        for zs, gs in A_PARTS:
            ea[half[h], zs, :, gs] = encode(sa[half[h], zs, :, gs], TOP / top)
        for k in ((1, 3), (2,))[h]:
            p, to = at_y(k)
            for q, (zs, gs) in enumerate(A_PARTS):
                rs2a[k, q] = send(ea.at[half[h], zs, yhl(p)[0], gs], ry2.at[y, zs, gs], to)
            rsu["y2", k] = send(u2.at[h], u2y.at[y], to)

    second_a(0)
    drain(early)
    second_a(1)
    top = jnp.full((8, 128), LEAST, F32)
    for k in range(1, Y):
        got(rsu["y", k], uy.at[at_y(-k)[0]])
    for q, (zs, gs, ls) in enumerate(B_PARTS):
        total = gall[c, yl, zs, yh, :, gs]
        for k in range(1, Y):
            src = at_y(-k)[0]
            got(rsb[k, q], ry1.at[src, zs, :, ls])
            total = total + decode(ry1[src, zs, :, ls], uy[src])
        sb[zs, :, ls] = total
        top = jnp.maximum(top, largest(total))
    u2[2] = top * (1.0 / TOP)
    for zs, gs, ls in B_PARTS:
        eb[zs, :, ls] = encode(sb[zs, :, ls], TOP / top)
    for k in range(1, X):
        p, to = at_x(k)
        for q, (zs, gs, ls) in enumerate(B_PARTS):
            rs2b[k, q] = send(eb.at[zs, p, ls], rx2.at[x, zs, ls], to)
        rsu["x2", k] = send(u2.at[2], u2x.at[x], to)
    got(bias_core, bb.at[1 - c])
    bx[x] = bb[0] + bb[1]
    bias_x = [send(bx.at[x], bx.at[x], at_x(k)[1]) for k in range(1, X)]

    early = len(sends)

    relay_a, relay_b = {}, {}

    def relay(ref):
        return send(ref, ref, sibling)

    for q in range(len(A_PARTS)):
        relay_a[0, q] = relay(a_slab(x, q, c))
    for q in range(len(B_PARTS)):
        relay_b[0, q] = relay(b_slab(y, q, c))
    for k in (1, 3, 2):
        for q in range(len(A_PARTS)):
            got(ag3a[k, q], a_slab(at_x(-k)[0], q, c))
            relay_a[k, q] = relay(a_slab(at_x(-k)[0], q, c))
        for q in range(len(B_PARTS)):
            got(ag3b[k, q], b_slab(at_y(-k)[0], q, c))
            relay_b[k, q] = relay(b_slab(at_y(-k)[0], q, c))
    for k in range(1, Z):
        got(ag3c[k], c_slab(at_z(-k)[0]), away(k)[0])
    c_all = lambda cc: wb.at[:, C_PLACES, cc, :, :, G3]
    relay_c = relay(c_all(c))

    for k in range(1, X):
        got(bias_x[k - 1], bx.at[at_x(-k)[0]])
    by[y] = (bx[0] + bx[1]) + (bx[2] + bx[3])
    bias_y = [send(by.at[y], by.at[y], at_y(k)[1]) for k in range(1, Y)]

    for k in range(1, Z):
        got(rsz[k], rz1.at[at_z(-k)[0]], even)
        got(rsu["z", k], uz.at[at_z(-k)[0]], even)

    @pl.when(even)
    def _():
        for h in range(2):
            total = gall[c, half[h], pz, :, :, G3]
            for k in range(1, Z):
                src = at_z(-k)[0]
                total = total + decode(rz1[src, half[h]], uz[src, h])
            sc[half[h]] = total

    for k in range(1, X):
        p, to = at_x(k)
        rsc2[k] = send(sc.at[:, :, p], rc2.at[x], to, even)

    drain(early)

    @pl.loop(0, 2 * Z)
    def _(i):
        pltpu.make_async_remote_copy(
            src_ref=gr.at[0, 0], dst_ref=gr.at[0, 0], send_sem=dsem.at[i], recv_sem=drsem.at[i],
            device_id=sibling, device_id_type=MESH,
        ).wait_send()

    for k in range(1, Y):
        got(rsu["y2", k], u2y.at[at_y(-k)[0]])
    for q, (zs, gs) in enumerate(A_PARTS):
        total = sa[yl, zs, yh, gs]
        for k in range(1, Y):
            src = at_y(-k)[0]
            got(rs2a[k, q], ry2.at[src, zs, gs])
            total = total + decode(ry2[src, zs, gs], u2y[src])
        s2[zs, gs] = total
    for k in range(1, X):
        got(rsu["x2", k], u2x.at[at_x(-k)[0]])
    for q, (zs, gs, ls) in enumerate(B_PARTS):
        total = sb[zs, x, ls]
        for k in range(1, X):
            src = at_x(-k)[0]
            got(rs2b[k, q], rx2.at[src, zs, ls])
            total = total + decode(rx2[src, zs, ls], u2x[src])
        s2[zs, gs] = total
    rs3, rs3o, rsc3 = {}, {}, {}
    first3 = pl.ds(0, 3)
    for k in range(1, Z):
        p, to = at_z(k)
        place = reversed_bits(p)
        rs3[k] = send(s2.at[place, first3], rz3.at[z, first3], to)
        rs3o[k] = send(s2.at[place, G3], rz3.at[z, G3], to, away(k)[1])
    for k in range(1, X):
        got(rsc2[k], rc2.at[at_x(-k)[0]], even)

    @pl.when(even)
    def _():
        total = sc[:, :, x]
        for k in range(1, X):
            total = total + rc2[at_x(-k)[0]]
        sc2[...] = total

    for k in range(1, Y):
        p, to = at_y(k)
        ph, pw = yhl(p)
        rsc3[k] = send(sc2.at[pw, ph], rc3.at[y], to, even)
    for k in range(X):
        for q in range(len(A_PARTS)):
            got(relay_a[k, q], a_slab(at_x(-k)[0], q, 1 - c))
        for q in range(len(B_PARTS)):
            got(relay_b[k, q], b_slab(at_y(-k)[0], q, 1 - c))
    got(relay_c, c_all(1 - c))
    acc[...] = jnp.broadcast_to(bias_ref[...], acc.shape)

    def products(lo, hi):
        @pl.loop(lo, hi)
        def _(j):
            q = lax.rem(j, 4)
            p = lax.rem(q, 2) * 2 + q // 2
            w = jnp.concatenate(
                [
                    jnp.concatenate(
                        [wb[j // 4, p + d, :, :, :, g].reshape(256, 128) for d in (0, 4)], axis=0
                    )
                    for g in range(4)
                ],
                axis=1,
            )
            cols = pl.ds(pl.multiple_of(j * 512, 512), 512)
            gto[:, cols] = lax.dot_general(
                gv[...], w, (((1,), (1,)), ((), ())), preferred_element_type=F32
            ).astype(BF16)
            acc[...] += jnp.dot(tok[:, cols], w, preferred_element_type=F32)

    products(0, 4)

    for k in range(1, Y):
        got(bias_y[k - 1], by.at[at_y(-k)[0]])
    bz[z] = (by[0] + by[1]) + (by[2] + by[3])
    bias_z = [send(bz.at[z], bz.at[z], at_z(k)[1]) for k in range(1, Z)]
    products(4, 8)
    valo[...] = acc[...].astype(BF16)

    for k in range(1, Z):
        got(bias_z[k - 1], bz.at[at_z(-k)[0]])
    total = bz[0]
    for k in range(1, Z):
        total = total + bz[k]
    gb_ref[...] = total[0:1] * scale
    for k in range(1, Y):
        got(rsc3[k], rc3.at[at_y(-k)[0]], even)

    @pl.when(even)
    def _():
        total = sc2[yl, yh, 0]
        for k in range(1, Y):
            total = total + rc3[at_y(-k)[0], 0]
        gw_ref[:, pl.ds(384, 128)] = total

    for k in range(1, Z):
        got(rs3[k], rz3.at[at_z(-k)[0], first3])
        got(rs3o[k], rz3.at[at_z(-k)[0], G3], odd)
    total = s2[pz, first3]
    for k in range(1, Z):
        total = total + rz3[at_z(-k)[0], first3]
    for g in range(3):
        gw_ref[:, pl.ds(g * 128, 128)] = total[g]

    @pl.when(odd)
    def _():
        total = s2[pz, 3]
        for k in range(1, Z):
            total = total + rz3[at_z(-k)[0], 3]
        gw_ref[:, pl.ds(384, 128)] = total

    drain(len(sends))
    assert count[0] <= N_SEM, count[0]


def write_kernel(val, gt, gw, gb, val_out, gt_out, gw_out, gb_out, sem):
    copies = [pltpu.make_async_copy(val, val_out, sem.at[0])]
    rows = gt.shape[0] // 4
    for q in range(4):
        part = pl.ds(q * rows, rows)
        copies.append(pltpu.make_async_copy(gt.at[part], gt_out.at[part], sem.at[1 + q]))
    copies.append(pltpu.make_async_copy(gw, gw_out, sem.at[5]))
    copies.append(pltpu.make_async_copy(gb, gb_out, sem.at[6]))
    for cp_ in copies:
        cp_.start()
    for cp_ in copies:
        cp_.wait()


def shards(tokens, weight, bias, grad_values):
    rows, width = tokens.shape
    feats = weight.shape[1]
    n = lax.axis_size("outer") * lax.axis_size("inner")
    scale = float(1.0 / (rows * n) ** 0.5)
    anyspace = pl.BlockSpec(memory_space=pl.ANY)
    vmem = pl.BlockSpec(memory_space=pltpu.VMEM)
    tile = (16, 128)
    scratch = [
        ((rows, width), BF16),
        ((rows, feats), BF16),
        ((2, Z, 2, 2, X, 4) + tile, BF16),
        ((2, 2, Z, 2, X, 4) + tile, F32),
        ((2, Z, 2, X, 4) + tile, F32),
        ((rows, feats), F32),
        ((X, 2, Z, 2, 2) + tile, BF16),
        ((Y, Z, X, 3) + tile, BF16),
        ((Z, 2, 2, X, 1) + tile, BF16),
        ((2, Z, 2, 2) + tile, F32),
        ((Z, X, 3) + tile, F32),
        ((2, 2, X, 1) + tile, F32),
        ((Y, Z, 2) + tile, BF16),
        ((X, Z, 3) + tile, BF16),
        ((X, 2, 2, 1) + tile, F32),
        ((Z, 4) + tile, F32),
        ((2, 2, 1) + tile, F32),
        ((Z, 4) + tile, F32),
        ((Y, 1) + tile, F32),
        ((2, Z, 2, X, 4) + tile, BF16),
        ((2, Z, 2, 2) + tile, BF16),
        ((Z, X, 3) + tile, BF16),
        ((2, 8, 128), F32),
        ((X, 2, 8, 128), F32),
        ((Y, 8, 128), F32),
        ((Z, 2, 8, 128), F32),
        ((3, 8, 128), F32),
        ((Y, 8, 128), F32),
        ((X, 8, 128), F32),
        ((2, 8, feats), F32),
        ((X, 8, feats), F32),
        ((Y, 8, feats), F32),
        ((Z, 8, feats), F32),
    ]
    dma = pltpu.SemaphoreType.DMA
    outs = (
        ((rows, feats), BF16),
        ((rows, width), BF16),
        (weight.shape, F32),
        ((1, feats), F32),
    )
    results = pl.pallas_call(
        functools.partial(kernel, scale),
        out_shape=tuple(pltpu.VMEM(s, d) for s, d in outs),
        in_specs=[anyspace, anyspace, vmem, anyspace],
        out_specs=(vmem,) * 4,
        scratch_shapes=[pltpu.VMEM(s, d) for s, d in scratch]
        + [dma((N_SEM,)), dma((N_SEM,)), dma((2 * Z,)), dma((2 * Z,)), dma((8,))],
        compiler_params=pltpu.CompilerParams(
            collective_id=0, has_side_effects=True, vmem_limit_bytes=50 * 1024 * 1024
        ),
        cost_estimate=pl.CostEstimate(
            flops=6 * rows * width * feats, bytes_accessed=4 * rows * width, transcendentals=0
        ),
        name="gather_scatter",
    )(tokens, weight, bias.reshape(1, feats), grad_values)
    values, grad_tokens, grad_weight, grad_bias = pl.pallas_call(
        write_kernel,
        out_shape=tuple(jax.ShapeDtypeStruct(s, d) for s, d in outs),
        in_specs=[vmem] * 4,
        out_specs=(anyspace,) * 4,
        scratch_shapes=[dma((8,))],
        compiler_params=pltpu.CompilerParams(vmem_limit_bytes=1024 * 1024),
        name="write",
    )(*[pltpu.with_memory_space_constraint(r, pltpu.VMEM) for r in results])
    return values, grad_tokens, grad_weight, grad_bias.reshape(feats)


def solution(mesh):
    in_specs = (
        P(("outer", "inner"), None),
        P(("outer", "inner"), None),
        P(),
        P(("outer", "inner"), None),
    )
    out_specs = (
        P(("outer", "inner"), None),
        P(("outer", "inner"), None),
        P(("outer", "inner"), None),
        P(),
    )
    return jax.shard_map(shards, mesh=mesh, in_specs=in_specs, out_specs=out_specs, check_vma=False)
```
